128 devices in a mesh: ep: 128 (over z, y, x, core).
Axes of the slice: x: 4, y: 4, z: 4, core: 2. Of those that a mesh axis runs over, the one named last changes fastest.
Arguments:
- tokens: bfloat16 [16384, 1024], P('ep'), may hold values from -6 to 6
- cotangent: bfloat16 [16384, 1024], P('ep'), may hold values from -6 to 6
- routes: int32 [16384, 8], P('ep'), may hold values from 0 to 127, all different within a row; in each aligned block of 128 rows (0 to 127, 128 to 255, ...) at most 12 rows name the same one
- gate_weights: float32 [16384, 8], P('ep'), may hold values from 0.05 to 0.5
- old_experts: int32 [128], replicated, may hold values from 0 to 63
- source: int32 [128], replicated, may hold values from 0 to 127
- gate_up_weight: bfloat16 [128, 1024, 1024], P('ep'), may hold values from -0.1875 to 0.1875
- down_weight: bfloat16 [128, 512, 1024], P('ep'), may hold values from -0.25 to 0.25
- first_gate_up: bfloat16 [128, 1024, 1024], P('ep'), may hold values from -18 to 18
- first_down: bfloat16 [128, 512, 1024], P('ep'), may hold values from -18 to 18
- second_gate_up: bfloat16 [128, 1024, 1024], P('ep'), may hold values from 1 to 100
- second_down: bfloat16 [128, 512, 1024], P('ep'), may hold values from 1 to 100
Outputs:
- layer_out: bfloat16 [16384, 1024], P('ep')
- new_gate_up: bfloat16 [128, 1024, 1024], P('ep')
- new_down: bfloat16 [128, 512, 1024], P('ep')
- new_first_gate_up: bfloat16 [128, 1024, 1024], P('ep')
- new_first_down: bfloat16 [128, 512, 1024], P('ep')
- new_second_gate_up: bfloat16 [128, 1024, 1024], P('ep')
- new_second_down: bfloat16 [128, 512, 1024], P('ep')
The draws below stay inside these ranges and needn't reach their ends.
Inputs may be any that keep to these rules, and one draw needn't show every extreme that they name: `routes`: the 8 slots of a token differ; among the rows of one device no slot is named more than 12 times, a bound that some block reaches.
All inputs are finite; a program needn't handle non-finite values.
Results may differ from the reference program's by a relative error of at most 0.0058.
Values may be sent and summed in bfloat16 or wider, within the bound.
A program may use at most 128 MiB of HBM per device.

```python
import math
import jax
import jax.numpy as jnp
import numpy as np
from jax import lax

D = 1024
FF = 512
EXPERTS = 64
TOP = 8
TOK_DEV = 128
SLOTS = 128
TOKENS = 16384
CAP = 12
N_EP = 128


def touch_ends(array, own_key, smallest, top_value):
    index_at = [jax.random.randint(jax.random.fold_in(own_key, axis), (), 0, length) for axis, length in enumerate(array.shape)]
    widest = array.shape.index(max(array.shape))
    beside = index_at[:widest] + [(index_at[widest] + 1) % array.shape[widest]] + index_at[widest + 1:]
    return array.at[tuple(index_at)].set(smallest).at[tuple(beside)].set(top_value)


def steps_of(stream_key, dims, cuts, smallest, high):
    def one(dim, parts):
        heights = jax.random.uniform(jax.random.fold_in(jax.random.fold_in(stream_key, 6), dim), (parts,), jnp.float32, smallest / len(cuts), high / len(cuts))
        return jnp.repeat(jnp.exp(heights), dims[dim] // parts).reshape((-1,) + (1,) * (len(dims) - dim - 1))

    factor_of = one(*cuts[0])
    for cut in cuts[1:]:
        factor_of = factor_of * one(*cut)
    return factor_of


def assign_block(key, own, number, rows, amount, top, limit, lean):
    ranking = jax.random.permutation(key, amount)
    heavy_load, ordinary = portions_of(amount, rows * top, limit, lean, True), portions_of(amount, rows * top, limit, lean, False)
    places = jnp.arange(amount)

    def named(tallies, turn):
        used = int((tallies > 0).sum())
        fixed = max(1, used // 4)
        moved = fixed + (places - fixed + turn * (used - fixed)) % max(1, amount - fixed)
        return jnp.zeros((amount,), jnp.int32).at[ranking[jnp.where(places < fixed, places, moved)]].set(jnp.asarray(tallies, jnp.int32))

    tallies = jnp.where(number % 4 == 0, named(heavy_load, number // 4), named(ordinary, number - number // 4 - 1))
    mixed = jax.random.permutation(jax.random.fold_in(own, 3), amount)
    source_of, receiver = mixed[0:amount // 2 * 2:2], mixed[1:amount // 2 * 2:2]
    margin = jnp.minimum(tallies[source_of] - 1, limit - tallies[receiver]) // 2
    margin = jnp.where((source_of == ranking[0]) | (receiver == ranking[0]) | (tallies[receiver] == 0), 0, jnp.maximum(margin, 0))
    moved = jax.random.randint(jax.random.fold_in(own, 4), (amount // 2,), 0, 1 << 20) % (margin + 1)
    tallies = tallies.at[source_of].add(-moved).at[receiver].add(moved)
    items = jnp.searchsorted(jnp.cumsum(tallies), jnp.arange(rows * top), side="right").astype(jnp.int32)
    table = items.reshape(top, rows).T
    table = table[jax.random.permutation(jax.random.fold_in(own, 1), rows)]
    turn = jax.random.randint(jax.random.fold_in(own, 2), (rows, 1), 0, top)
    return jnp.take_along_axis(table, (jnp.arange(top)[None, :] + turn) % top, axis=1)


def portions_of(count, total, most, slope, full):
    loads = [(1 << 20) // math.isqrt(rank ** slope) + 1 for rank in range(1, count + 1)]
    largest = most if full else min(most, max(-(-total // count), total * loads[0] // sum(loads)))
    least = 1 if total - largest >= count - 1 else 0
    given, rest = [largest] + [least] * (count - 1), total - largest - least * (count - 1)
    while rest > 0:
        movable = [i for i in range(1, count) if given[i] < largest] or [i for i in range(1, count) if given[i] < most]
        pool, budget = sum([loads[i] for i in movable]), rest
        for i in movable:
            extra = min(most - given[i], max(1, budget * loads[i] // pool), rest)
            given[i] = given[i] + extra
            rest = rest - extra
    return np.array(given)


def scatter_about(rng, dims, width, limit, cuts=(), kind=jnp.bfloat16):
    drawn = jax.random.normal(rng, dims, jnp.float32) * width
    if len(cuts) > 0:
        drawn = steps_of(rng, dims, cuts, -0.22, 0.18) * drawn
    return jnp.clip(drawn, min=-limit, max=limit).astype(kind)


def setup_inputs(seed: int = 0) -> dict:
    streams_of = jax.random.split(jax.random.key(seed), 13)
    tokens = scatter_about(streams_of[0], (TOKENS, D), 1.0, 6.0, ((0, 128),))
    cotangent = scatter_about(streams_of[1], (TOKENS, D), 1.0, 6.0, ((0, 128),))
    routes_keys = jax.random.split(jax.random.fold_in(streams_of[2], 1), TOKENS // TOK_DEV)
    routes_turns = jax.random.permutation(jax.random.fold_in(streams_of[2], 3), TOKENS // TOK_DEV)
    routes = jax.vmap(lambda own, number: assign_block(jax.random.fold_in(streams_of[2], 2), own, number, TOK_DEV, SLOTS, TOP, CAP, 2))(routes_keys, routes_turns).reshape((TOKENS, TOP))
    gate_weights = jnp.clip(jnp.exp(math.log(0.5) - 2.3025851 * jax.random.uniform(streams_of[3], (TOKENS, TOP), jnp.float32) ** steps_of(streams_of[3], (TOKENS, TOP), ((0, 128),), -0.2, 0.2)), 0.05, 0.5)
    old_experts = touch_ends(jax.random.randint(streams_of[4], (SLOTS,), 0, EXPERTS), jax.random.fold_in(streams_of[4], 1), 0, EXPERTS - 1).astype(jnp.int32)
    source = touch_ends(jax.random.randint(streams_of[5], (SLOTS,), 0, SLOTS), jax.random.fold_in(streams_of[5], 1), 0, SLOTS - 1).astype(jnp.int32)
    gate_up_weight = scatter_about(streams_of[6], (SLOTS, D, 2 * FF), D ** -0.5, 0.1875, ((0, 128),))
    down_weight = scatter_about(streams_of[7], (SLOTS, FF, D), FF ** -0.5, 0.25, ((0, 128),))
    first_gate_up = scatter_about(streams_of[8], (SLOTS, D, 2 * FF), 3.0, 18.0, ((0, 128),))
    first_down = scatter_about(streams_of[9], (SLOTS, FF, D), 3.0, 18.0, ((0, 128),))
    second_gate_up = jnp.clip(jnp.exp(math.log(100.0) - 4.6051702 * jax.random.uniform(streams_of[10], (SLOTS, D, 2 * FF), jnp.float32) ** steps_of(streams_of[10], (SLOTS, D, 2 * FF), ((0, 128),), -0.2, 0.2)), 1.0, 100.0).astype(jnp.bfloat16)
    second_down = jnp.clip(jnp.exp(math.log(100.0) - 4.6051702 * jax.random.uniform(streams_of[11], (SLOTS, FF, D), jnp.float32) ** steps_of(streams_of[11], (SLOTS, FF, D), ((0, 128),), -0.2, 0.2)), 1.0, 100.0).astype(jnp.bfloat16)
    return {"tokens": tokens, "cotangent": cotangent, "routes": routes, "gate_weights": gate_weights, "old_experts": old_experts, "source": source, "gate_up_weight": gate_up_weight, "down_weight": down_weight, "first_gate_up": first_gate_up, "first_down": first_down, "second_gate_up": second_gate_up, "second_down": second_down}


def positions(flat_routes, n_slots):
    onehot = (flat_routes[:, None] == jnp.arange(n_slots, dtype=jnp.int32)[None, :]).astype(jnp.int32)
    before = jnp.cumsum(onehot, axis=0) - onehot
    return lax.optimization_barrier(jnp.sum(before * onehot, axis=1)).astype(jnp.int32)

def forward_backward(rows_x, rows_dy, gate_up, down_part):
    hidden_width = down_part.shape[0]
    pre_act = jnp.dot(rows_x, gate_up, preferred_element_type=jnp.float32)
    gate_pre = pre_act[:, :hidden_width]
    up_part = pre_act[:, hidden_width:]
    sigmoid_gate = jax.nn.sigmoid(gate_pre)
    activated = gate_pre * sigmoid_gate
    hidden = (activated * up_part).astype(jnp.bfloat16)
    output = jnp.dot(hidden, down_part, preferred_element_type=jnp.float32).astype(jnp.bfloat16)
    d_hidden = jnp.dot(rows_dy, down_part.T, preferred_element_type=jnp.float32)
    d_gate = d_hidden * up_part * sigmoid_gate * (1.0 + gate_pre * (1.0 - sigmoid_gate))
    d_up = d_hidden * activated
    d_pre = jnp.concatenate([d_gate, d_up], axis=1).astype(jnp.bfloat16)
    grad_gate_up = jnp.dot(rows_x.T, d_pre, preferred_element_type=jnp.float32)
    grad_down = jnp.dot(hidden.T, rows_dy, preferred_element_type=jnp.float32)
    return (output, grad_gate_up, grad_down)

def adam_update(weight, first_moment, second_moment, gradient):
    first_new = 0.9 * first_moment.astype(jnp.float32) + 0.1 * gradient
    second_new = 0.95 * second_moment.astype(jnp.float32) + 0.05 * gradient * gradient
    weight_new = weight.astype(jnp.float32) - 0.01 * first_new / (jnp.sqrt(second_new) + 1e-08)
    return (weight_new.astype(jnp.bfloat16), first_new.astype(jnp.bfloat16), second_new.astype(jnp.bfloat16))

def reference(tokens, cotangent, routes, gate_weights, old_experts, source, gate_up_weight, down_weight, first_gate_up, first_down, second_gate_up, second_down):
    n_slots = SLOTS
    block_routes = routes.reshape(N_EP, TOK_DEV * TOP)
    position = jax.vmap(lambda one_block: positions(one_block, n_slots))(block_routes)
    block_ids = jnp.arange(N_EP, dtype=jnp.int32)[:, None]
    rows_in_slot = (block_ids * CAP + position).reshape(-1).astype(jnp.int32)
    flat_slot = routes.reshape(-1).astype(jnp.int32)
    assign_ids = jnp.arange(TOKENS * TOP, dtype=jnp.int32)
    slot_table = jnp.full((n_slots, N_EP * CAP), -1, jnp.int32).at[flat_slot, rows_in_slot].set(assign_ids)
    flat_gates = gate_weights.reshape(-1)
    new_expert = old_experts[source]

    def per_slot(running, slot_id):
        layer_acc, grad_gu_acc, grad_dn_acc = running
        assign_index = slot_table[slot_id]
        is_valid = assign_index >= 0
        safe_index = jnp.where(is_valid, assign_index, 0)
        token_id = safe_index // TOP
        rows_x = jnp.where(is_valid[:, None], tokens[token_id], jnp.zeros((), tokens.dtype))
        gate_scale = jnp.where(is_valid, flat_gates[safe_index], jnp.zeros((), flat_gates.dtype))
        rows_dy = (gate_scale[:, None] * cotangent[token_id].astype(jnp.float32)).astype(jnp.bfloat16)
        src_slot = source[slot_id]
        output, grad_gu, grad_dn = forward_backward(rows_x, rows_dy, gate_up_weight[src_slot], down_weight[src_slot])
        layer_acc = layer_acc.at[token_id].add(gate_scale[:, None] * output.astype(jnp.float32))
        expert = new_expert[slot_id]
        grad_gu_acc = grad_gu_acc.at[expert].add(grad_gu)
        grad_dn_acc = grad_dn_acc.at[expert].add(grad_dn)
        return ((layer_acc, grad_gu_acc, grad_dn_acc), None)
    start = (jnp.zeros((TOKENS, D), jnp.float32), jnp.zeros((EXPERTS, D, 2 * FF), jnp.float32), jnp.zeros((EXPERTS, FF, D), jnp.float32))
    (layer_acc, grad_gu_all, grad_dn_all), unused = lax.scan(per_slot, start, jnp.arange(n_slots, dtype=jnp.int32))
    layer_out = layer_acc.astype(jnp.bfloat16)

    def finish(slot_id):
        src_slot = source[slot_id]
        expert = new_expert[slot_id]
        gate_new = adam_update(gate_up_weight[src_slot], first_gate_up[src_slot], second_gate_up[src_slot], grad_gu_all[expert])
        down_new = adam_update(down_weight[src_slot], first_down[src_slot], second_down[src_slot], grad_dn_all[expert])
        return (gate_new[0], down_new[0], gate_new[1], down_new[1], gate_new[2], down_new[2])
    results = lax.map(finish, jnp.arange(n_slots, dtype=jnp.int32))
    return (layer_out, results[0], results[1], results[2], results[3], results[4], results[5])
```

```python
import jax
import jax.numpy as jnp
from jax import lax
from jax.sharding import PartitionSpec as P

N = 128
CAP = 12
BF = jnp.bfloat16
F32 = jnp.float32


def exchange(x):
    return lax.all_to_all(x, "ep", split_axis=0, concat_axis=0, tiled=True)


def pack(gate_up, down):
    a = gate_up.reshape(32, 32, 4, 256).transpose(0, 2, 1, 3).reshape(N, 32, 256)
    b = down.reshape(32, 16, 4, 256).transpose(0, 2, 1, 3).reshape(N, 16, 256)
    return jnp.concatenate([a, b], axis=1)


def unpack(pieces):
    a = pieces[:, :32].reshape(32, 4, 32, 256).transpose(0, 2, 1, 3).reshape(1024, 1024)
    b = pieces[:, 32:48].reshape(32, 4, 16, 256).transpose(0, 2, 1, 3).reshape(512, 1024)
    return a, b


def shards(
    tokens,
    cotangent,
    routes,
    gate_weights,
    old_experts,
    source,
    gate_up_weight,
    down_weight,
    first_gate_up,
    first_down,
    second_gate_up,
    second_down,
):
    w_pieces = exchange(pack(gate_up_weight[0], down_weight[0]))

    slots = jnp.arange(N, dtype=jnp.int32)
    named = routes[:, :, None] == slots
    hit = jnp.any(named, axis=1)
    gate_of = jnp.sum(jnp.where(named, gate_weights[:, :, None], 0.0), axis=1)
    below = (slots[:, None] > slots[None, :]).astype(BF)
    row = jnp.dot(below, hit.astype(BF), preferred_element_type=F32)
    row = jnp.where(hit, row, -1.0)
    ranks = jnp.arange(CAP, dtype=F32)
    place = (row.T[:, None, :] == ranks[None, :, None]).astype(BF)
    place = place.reshape(N * CAP, N)
    place_gate = jnp.sum(
        jnp.where(row.T[:, None, :] == ranks[None, :, None], gate_of.T[:, None, :], 0.0), axis=2
    ).reshape(N * CAP, 1)
    send_x = jnp.dot(place, tokens, preferred_element_type=F32).astype(BF)
    send_c = jnp.dot(place, cotangent, preferred_element_type=F32)
    send_dy = (place_gate * send_c).astype(BF)
    send = jnp.concatenate(
        [send_x.reshape(N, CAP, 1024), send_dy.reshape(N, CAP, 1024)], axis=1
    )
    rows = exchange(send)
    rows_x = rows[:, :CAP].reshape(N * CAP, 1024)
    rows_dy = rows[:, CAP:].reshape(N * CAP, 1024)

    w_home = exchange(jnp.take(w_pieces, source, axis=0))
    gate_up, down = unpack(w_home)

    state = jnp.concatenate(
        [pack(first_gate_up[0], first_down[0]), pack(second_gate_up[0], second_down[0])], axis=1
    )
    state_pieces = exchange(state)

    pre = jnp.dot(rows_x, gate_up, preferred_element_type=F32)
    gate_pre = pre[:, :512]
    up = pre[:, 512:]
    sig = jax.nn.sigmoid(gate_pre)
    act = gate_pre * sig
    hidden = (act * up).astype(BF)
    out = jnp.dot(hidden, down, preferred_element_type=F32).astype(BF)
    d_hidden = jnp.dot(rows_dy, down.T, preferred_element_type=F32)
    d_gate = d_hidden * up * sig * (1.0 + gate_pre * (1.0 - sig))
    d_up = d_hidden * act
    d_pre = jnp.concatenate([d_gate, d_up], axis=1).astype(BF)
    grad_gu = jnp.dot(rows_x.T, d_pre, preferred_element_type=F32).astype(BF)
    grad_dn = jnp.dot(hidden.T, rows_dy, preferred_element_type=F32).astype(BF)

    back = exchange(
        jnp.concatenate(
            [
                out.reshape(N, CAP, 4, 256).transpose(0, 2, 1, 3).reshape(N, 48, 256),
                pack(grad_gu, grad_dn),
            ],
            axis=1,
        )
    )
    returned = back[:, :48].reshape(N, 4, CAP, 256).transpose(0, 2, 1, 3).reshape(N * CAP, 1024)
    grads = back[:, 48:]

    new_expert = old_experts[source]
    same = (new_expert[:, None] == new_expert[None, :]).astype(BF)
    total = jnp.einsum("sr,rjc->sjc", same, grads, preferred_element_type=F32)
    chosen = jnp.take(state_pieces, source, axis=0)
    first_new = (0.9 * chosen[:, :48].astype(F32) + 0.1 * total).astype(BF)
    second_new = (0.95 * chosen[:, 48:].astype(F32) + 0.05 * total * total).astype(BF)
    final = exchange(jnp.concatenate([first_new, second_new], axis=1))

    gate_hi = place_gate.astype(BF)
    gate_lo = (place_gate - gate_hi.astype(F32)).astype(BF)
    combine = jnp.concatenate([place * gate_hi, place * gate_lo], axis=1)
    mixed = lax.dot_general(
        combine, returned, (((0,), (0,)), ((), ())), preferred_element_type=F32
    )
    layer_out = (mixed[:N] + mixed[N:]).astype(BF)

    m_gu, m_dn = unpack(final[:, :48])
    q_gu, q_dn = unpack(final[:, 48:])

    def step(w, m, q):
        return (
            w.astype(F32) - 0.01 * m.astype(F32) / (jnp.sqrt(q.astype(F32)) + 1e-8)
        ).astype(BF)

    return (
        layer_out,
        step(gate_up, m_gu, q_gu)[None],
        step(down, m_dn, q_dn)[None],
        m_gu[None],
        m_dn[None],
        q_gu[None],
        q_dn[None],
    )


def solution(mesh):
    tok = P("ep", None)
    slot = P("ep", None, None)
    return jax.shard_map(
        shards,
        mesh=mesh,
        in_specs=(tok,) * 4 + (P(), P()) + (slot,) * 6,
        out_specs=(tok,) + (slot,) * 6,
        check_vma=False,
    )
```

```python
import jax
import jax.numpy as jnp
from jax import lax
from jax.sharding import PartitionSpec as P
from jax.experimental import pallas as pl
from jax.experimental.pallas import tpu as pltpu

N = 128
CAP = 12
ROWS = N * CAP
BF = jnp.bfloat16
F32 = jnp.float32
MESH = pl.DeviceIdType.MESH

ORDER = (("x", "y", "z"), ("y", "z", "x"), ("z", "x", "y"))
BUF = (4, 4, 2, 16, 1024)


def coordinates():
    me = lax.axis_index("ep")
    return {"z": me // 32, "y": (me // 8) % 4, "x": (me // 2) % 4, "c": me % 2}


def device(at, **moved):
    q = {**at, **moved}
    return (q["z"] * 32 + q["y"] * 8 + q["x"] * 2 + q["c"],)


def cut(ref, rows, **kw):
    if "x" in kw:
        cols = pl.ds(pl.multiple_of(kw["x"] * 256, 256), 256)
    else:
        cols = slice(None)
    every = slice(None)
    row = every if rows is None else pl.ds(rows, 16)
    return ref.at[kw.get("z", every), kw.get("y", every), kw.get("c", every), row, cols]


def bounce_shape(stream, phase):
    size = {"z": 4, "y": 4, "c": 2, "x": 4}
    size[ORDER[stream][phase]] = None
    if phase == 0:
        size["c"] = None
    lead = tuple(size[a] for a in "zyc" if size[a])
    return lead + (16, 1024 if size["x"] else 256)


def enter(at):
    bar = pltpu.get_barrier_semaphore()
    pl.semaphore_signal(bar, inc=1, device_id=device(at, c=1 - at["c"]), device_id_type=MESH)
    for axis in "zyx":
        for d in (1, 2, 3):
            for dc in (0, 1):
                there = {axis: (at[axis] + d) % 4, "c": (at["c"] + dc) % 2}
                pl.semaphore_signal(
                    bar, inc=1, device_id=device(at, **there), device_id_type=MESH
                )
    pl.semaphore_wait(bar, 19)


class Exchanges:
    def __init__(self, at, stages, sends, receives, bounces, bounce_sems):
        self.at, self.stages = at, stages
        self.sends, self.receives = sends, receives
        self.bounces, self.bounce_sems = bounces, bounce_sems
        self.slots = len(bounces) // 9
        self.held = {}
        self.done = {g: 0 for g in stages}
        self.ids = {g: i for i, g in enumerate(stages)}

    def start(self, g, phase):
        at, i = self.at, self.ids[g]
        loads = []
        for s in range(3):
            if phase:
                self._arrived(g, s, phase - 1)
            (src, src_rows), (dst, dst_rows) = self.stages[g][s][phase : phase + 2]
            axis = ORDER[s][phase]
            mine = {axis: at[axis]}
            if phase == 0:
                mine["c"] = at["c"]
            used = {v for k, v in self.held.items() if k[1:] == (s, phase)}
            slot = min(set(range(self.slots)) - used)
            self.held[g, s, phase] = slot
            n = slot * 9 + s * 3 + phase
            load = pltpu.make_async_copy(
                cut(src, src_rows, **mine), self.bounces[n], self.bounce_sems.at[n]
            )
            load.start()
            loads.append((load, n, cut(dst, dst_rows, **mine), s))
        for d in (2, 1, 3, 0):
            for dc in (0, 1) if phase == 0 else (0,):
                if d == 0 and dc == 0:
                    continue
                for s in range(3):
                    (src, src_rows), (dst, dst_rows) = self.stages[g][s][phase : phase + 2]
                    axis = ORDER[s][phase]
                    mine = {axis: at[axis]}
                    there = {axis: (at[axis] + d) % 4}
                    if phase == 0:
                        mine["c"] = at["c"]
                        there["c"] = (at["c"] + dc) % 2
                    pltpu.make_async_remote_copy(
                        cut(src, src_rows, **there),
                        cut(dst, dst_rows, **mine),
                        self.sends.at[i, s, phase],
                        self.receives.at[i, s, phase],
                        device_id=device(at, **there),
                        device_id_type=MESH,
                    ).start()
        for load, n, dst, s in loads:
            load.wait()
            pltpu.make_async_copy(
                self.bounces[n], dst, self.receives.at[i, s, phase]
            ).start()

    def _arrived(self, g, s, phase):
        dst, rows = self.stages[g][s][phase + 1]
        whole = cut(dst, rows)
        pltpu.make_async_copy(whole, whole, self.receives.at[self.ids[g], s, phase]).wait()
        del self.held[g, s, phase]

    def finish(self, g):
        for s in range(3):
            self._arrived(g, s, 2)

    def drain(self):
        for g, i in self.ids.items():
            for s in range(3):
                for phase in range(3):
                    ref, rows = self.stages[g][s][phase + 1]
                    row = slice(None) if rows is None else pl.ds(rows, 16)
                    sent = ref.at[:, :, :, row, pl.ds(0, 768 if phase else 896)]
                    pltpu.make_async_copy(sent, sent, self.sends.at[i, s, phase]).wait()


def to_pieces(back, rows48, store):
    stacked = jnp.concatenate([rows48[:, q * 256 : q * 256 + 256] for q in range(4)], axis=0)
    moved = jnp.dot(back, stacked, preferred_element_type=F32).astype(BF)
    for s in range(3):
        store(s, moved[s * 64 : s * 64 + 64].reshape(4, 16, 256))


def from_pieces(there, refs, g, x):
    parts = [
        refs[s][g // 2, pl.ds(2 * (g % 2), 2), :, :, pl.ds(x * 256, 256)].reshape(64, 256)
        for s in range(3)
    ]
    return jnp.dot(
        there, jnp.concatenate(parts, axis=0), preferred_element_type=F32
    ).astype(BF)


def relayout(there, refs, out):
    def body(g, carry):
        for x in range(4):
            moved = from_pieces(there, refs, g, x)
            at = pl.multiple_of(x * 384 + g * 48, 16)
            for q in range(4):
                out[pl.ds(at, 48), q * 256 : q * 256 + 256] = moved[q * 48 : q * 48 + 48]
        return carry

    lax.fori_loop(0, 8, body, 0)


def piece_of(ref, table, is_x, i):
    full = ref[table[0, i], table[1, i], table[2, i]].astype(F32)
    return sum(full[:, x * 256 : x * 256 + 256] * is_x[x, i] for x in range(4))


def first_kernel(*refs):
    source, source_x = refs[:2]
    refs = refs[1:]
    (place, place_gate, there, back, tokens, cotangent) = refs[1:7]
    w_gu, w_dn, m_gu, m_dn, q_gu, q_dn = refs[7:13]
    (home_gu, home_dn) = refs[13:15]
    out_m, out_q, out_y = refs[15:18], refs[18:21], refs[21:24]
    out_ggu, out_gdn = refs[24:26]
    mids = refs[26:62]
    scratch = refs[62:]
    w_land, w_stage = scratch[0:3], scratch[3:6]
    x_send, c_send = scratch[6:9], scratch[9:12]
    x_land, c_land = scratch[12:15], scratch[15:18]
    gu, dn, xs, cs, hidden, d_pre = scratch[18:24]
    sends, receives, bounce_sems, copy_sem = scratch[24:28]
    bounces = scratch[28:]

    def mid(i):
        return [(mids[i * 6 + s], None) for s in range(3)], [
            (mids[i * 6 + 3 + s], None) for s in range(3)
        ]

    def raw(a, b):
        return [(a, 0), (a, 16), (b, None)]

    def plain(group):
        return [(r, None) for r in group]

    ends = {
        "w1": (raw(w_gu, w_dn), plain(w_land)),
        "x": (plain(x_send), plain(x_land)),
        "dy": (plain(c_send), plain(c_land)),
        "w2": (plain(w_stage), raw(gu, dn)),
        "m": (raw(m_gu, m_dn), plain(out_m)),
        "q": (raw(q_gu, q_dn), plain(out_q)),
    }
    stages = {}
    for i, (g, (first, last)) in enumerate(ends.items()):
        one, two = mid(i)
        stages[g] = [(first[s], one[s], two[s], last[s]) for s in range(3)]

    at = coordinates()
    enter(at)
    ex = Exchanges(at, stages, sends, receives, bounces, bounce_sems)

    def dispatch(rows, gate, out):
        def body(g, carry):
            for x in range(4):
                r = pl.ds(pl.multiple_of(x * 384 + g * 48, 16), 48)
                got = jnp.dot(place[r], rows[...], preferred_element_type=F32)
                if gate is not None:
                    got = got * gate[r]

                def store(s, value, x=x):
                    out[s][g // 2, pl.ds(2 * (g % 2), 2), :, :, x * 256 : x * 256 + 256] = (
                        value.reshape(2, 2, 16, 256)
                    )

                to_pieces(back[...], got.astype(BF), store)
            return carry

        lax.fori_loop(0, 8, body, 0)

    def select():
        def body(i, carry):
            z, y, c = i // 8, (i // 2) % 4, i % 2
            for x in range(4):
                slot = z * 32 + y * 8 + x * 2 + c
                for s in range(3):
                    w_stage[s][z, y, c, :, x * 256 : x * 256 + 256] = piece_of(
                        w_land[s], source, source_x, slot
                    ).astype(BF)
            return carry

        lax.fori_loop(0, 32, body, 0)

    ex.start("w1", 0)
    ex.start("m", 0)
    dispatch(tokens, None, x_send)
    ex.start("w1", 1)
    ex.start("x", 0)
    dispatch(cotangent, place_gate, c_send)
    ex.start("w1", 2)
    ex.start("dy", 0)
    ex.start("x", 1)
    ex.finish("w1")
    select()
    ex.start("w2", 0)
    ex.start("dy", 1)
    ex.start("w2", 1)
    ex.start("x", 2)
    ex.start("w2", 2)
    ex.start("dy", 2)
    ex.start("m", 1)
    ex.start("q", 0)
    ex.finish("x")
    relayout(there[...], x_land, xs)
    ex.finish("w2")
    keep_gu = pltpu.make_async_copy(gu, home_gu, copy_sem.at[0])
    keep_dn = pltpu.make_async_copy(dn, home_dn, copy_sem.at[1])
    keep_gu.start()
    keep_dn.start()
    ex.finish("dy")
    relayout(there[...], c_land, cs)
    ex.start("q", 1)

    def forward(b, carry):
        r = pl.ds(pl.multiple_of(b * 192, 16), 192)
        pre = jnp.zeros((192, 1024), F32)
        for k in range(4):
            pre += jnp.dot(
                xs[r, k * 256 : k * 256 + 256],
                gu[k].reshape(256, 1024),
                preferred_element_type=F32,
            )
        gate, up = pre[:, :512], pre[:, 512:]
        d_hid = jnp.concatenate(
            [
                lax.dot_general(
                    cs[r],
                    dn[k].reshape(128, 1024),
                    (((1,), (1,)), ((), ())),
                    preferred_element_type=F32,
                )
                for k in range(4)
            ],
            axis=1,
        )
        sig = jax.nn.sigmoid(gate)
        act = gate * sig
        h = (act * up).astype(BF)
        hidden[r] = h
        d_pre[r, 0:512] = (d_hid * up * sig * (1.0 + gate * (1.0 - sig))).astype(BF)
        d_pre[r, 512:1024] = (d_hid * act).astype(BF)
        y = jnp.zeros((192, 1024), F32)
        for k in range(4):
            y += jnp.dot(
                h[:, k * 128 : k * 128 + 128],
                dn[k].reshape(128, 1024),
                preferred_element_type=F32,
            )
        y = y.astype(BF)
        x, half = b // 2, b % 2
        cols = pl.ds(pl.multiple_of(x * 256, 256), 256)
        for j in range(4):
            g = half * 4 + j

            def store(s, value):
                out_y[s][g // 2, pl.ds(2 * (j % 2), 2), :, :, cols] = value.reshape(2, 2, 16, 256)

            to_pieces(back[...], y[j * 48 : j * 48 + 48], store)
        return carry

    lax.fori_loop(0, 8, forward, 0)
    ex.start("m", 2)
    ex.start("q", 2)
    for k in range(4):
        got = lax.dot_general(
            xs[:, k * 256 : k * 256 + 256],
            d_pre[...],
            (((0,), (0,)), ((), ())),
            preferred_element_type=F32,
        )
        out_ggu[k] = got.astype(BF).reshape(4, 2, 32, 1024)
        got = lax.dot_general(
            hidden[:, k * 128 : k * 128 + 128],
            cs[...],
            (((0,), (0,)), ((), ())),
            preferred_element_type=F32,
        )
        out_gdn[k] = got.astype(BF).reshape(4, 2, 16, 1024)
    ex.finish("m")
    ex.finish("q")
    ex.drain()
    keep_gu.wait()
    keep_dn.wait()


def second_kernel(*refs):
    source, source_x, order, order_x = refs[:4]
    refs = refs[2:]
    (last, keep, there, combine) = refs[2:6]
    g_gu, g_dn = refs[6:8]
    y_send, m_in, q_in = refs[8:11], refs[11:14], refs[14:17]
    layer_out = refs[17]
    new_m, new_q = refs[18:20], refs[20:22]
    mids = refs[22:46]
    scratch = refs[46:]
    g_land, y_land = scratch[0:3], scratch[3:6]
    m_old, q_old, m_send, q_send = (
        scratch[6:9],
        scratch[9:12],
        scratch[12:15],
        scratch[15:18],
    )
    sums, ys = scratch[18:20]
    sends, receives, bounce_sems, copy_sem = scratch[20:24]
    bounces = scratch[24:]

    def plain(group):
        return [(r, None) for r in group]

    def raw(a, b):
        return [(a, 0), (a, 16), (b, None)]

    ends = {
        "g": (raw(g_gu, g_dn), plain(g_land)),
        "y": (plain(y_send), plain(y_land)),
        "m": (plain(m_send), raw(*new_m)),
        "q": (plain(q_send), raw(*new_q)),
    }
    stages = {}
    for i, (g, (first, end)) in enumerate(ends.items()):
        stages[g] = [
            (first[s], (mids[i * 6 + s], None), (mids[i * 6 + 3 + s], None), end[s])
            for s in range(3)
        ]
    at = coordinates()
    enter(at)
    ex = Exchanges(at, stages, sends, receives, bounces, bounce_sems)
    ex.start("g", 0)
    ex.start("y", 0)
    fetch = [
        pltpu.make_async_copy(a, b, copy_sem.at[i])
        for i, (a, b) in enumerate(zip(m_in + q_in, m_old + q_old))
    ]
    for f in fetch:
        f.start()
    ex.start("g", 1)
    ex.start("y", 1)
    ex.start("g", 2)
    ex.finish("g")

    def running(i, acc):
        new = []
        for s in range(3):
            part = piece_of(g_land[s], order, order_x, i)
            new.append(acc[s] * keep[i] + part)
            sums[s, i] = new[s]
        return tuple(new)

    lax.fori_loop(0, N, running, (jnp.zeros((16, 256), F32),) * 3)
    ex.start("y", 2)
    for f in fetch:
        f.wait()

    def update(old, out, rule):
        def body(i, carry):
            z, y, c = i // 8, (i // 2) % 4, i % 2
            for x in range(4):
                slot = z * 32 + y * 8 + x * 2 + c
                e = last[slot]
                for s in range(3):
                    was = piece_of(old[s], source, source_x, slot)
                    out[s][z, y, c, :, x * 256 : x * 256 + 256] = rule(was, sums[s, e]).astype(BF)
            return carry

        lax.fori_loop(0, 32, body, 0)

    update(m_old, m_send, lambda was, t: 0.9 * was + 0.1 * t)
    ex.start("m", 0)
    update(q_old, q_send, lambda was, t: 0.95 * was + 0.05 * t * t)
    ex.start("q", 0)
    ex.start("m", 1)
    ex.finish("y")
    relayout(there[...], y_land, ys)
    mixed = lax.dot_general(
        combine[...], ys[...], (((1,), (0,)), ((), ())), preferred_element_type=F32
    )
    layer_out[...] = (mixed[:N] + mixed[N:]).astype(BF)
    ex.start("q", 1)
    ex.start("m", 2)
    ex.start("q", 2)
    ex.finish("m")
    ex.finish("q")
    ex.drain()


def shape(*dims, dtype=BF):
    return jax.ShapeDtypeStruct(dims, dtype)


def semaphores(groups, slots):
    dma = pltpu.SemaphoreType.DMA
    return [dma((groups, 3, 3)), dma((groups, 3, 3)), dma((slots * 9,)), dma((8,))]


def bounce_buffers(slots):
    return [
        pltpu.VMEM(bounce_shape(s, phase), BF)
        for _ in range(slots)
        for s in range(3)
        for phase in range(3)
    ]


def shards(
    tokens,
    cotangent,
    routes,
    gate_weights,
    old_experts,
    source,
    gate_up_weight,
    down_weight,
    first_gate_up,
    first_down,
    second_gate_up,
    second_down,
):
    seen = jnp.arange(N, dtype=jnp.int32)
    slots = (seen % 32) // 8 * 32 + (seen % 8) // 2 * 8 + seen // 32 * 2 + seen % 2
    named = routes[:, :, None] == slots
    hit = jnp.any(named, axis=1)
    gate_of = jnp.sum(jnp.where(named, gate_weights[:, :, None], 0.0), axis=1)
    below = (seen[:, None] > seen[None, :]).astype(BF)
    row = jnp.dot(below, hit.astype(BF), preferred_element_type=F32)
    row = jnp.where(hit, row, -1.0).T
    ranks = jnp.arange(CAP, dtype=F32)
    at_rank = row[:, None, :] == ranks[None, :, None]
    place = at_rank.astype(BF).reshape(ROWS, N)
    weighed = jnp.where(at_rank, gate_of.T[:, None, :], 0.0).reshape(ROWS, N)
    place_gate = jnp.sum(weighed, axis=1, keepdims=True)
    high = weighed.astype(BF)
    low = (weighed - high.astype(F32)).astype(BF)
    combine = jnp.concatenate([high, low], axis=1).T

    index = jnp.arange(192, dtype=jnp.int32)
    flat = index // 64 * 16 + index % 16
    where_to = flat // 12 * 48 + (index % 64) // 16 * 12 + flat % 12
    there = (index[:, None] == where_to[None, :]).astype(BF)
    back = there.T

    new_expert = old_experts[source]
    order = jnp.argsort(new_expert, stable=True).astype(jnp.int32)
    sorted_expert = new_expert[order]
    keep = jnp.concatenate(
        [jnp.zeros((1,), F32), (sorted_expert[1:] == sorted_expert[:-1]).astype(F32)]
    )
    last = jnp.sum((sorted_expert[None, :] <= new_expert[:, None]).astype(jnp.int32), axis=1) - 1

    def places(device):
        is_x = ((device // 2) % 4)[None, :] == jnp.arange(4)[:, None]
        lead = jnp.stack([device // 32, (device // 8) % 4, device % 2]).astype(jnp.int32)
        return lead, is_x.astype(F32)

    (source, source_x), (order, order_x) = places(source), places(order)
    gu_shape, dn_shape = (4, 4, 2, 32, 1024), BUF
    arrays = (
        gate_up_weight.reshape(gu_shape),
        down_weight.reshape(dn_shape),
        first_gate_up.reshape(gu_shape),
        first_down.reshape(dn_shape),
        second_gate_up.reshape(gu_shape),
        second_down.reshape(dn_shape),
    )
    smem = pl.BlockSpec(memory_space=pltpu.SMEM)
    vmem = pl.BlockSpec(memory_space=pltpu.VMEM)
    hbm = pl.BlockSpec(memory_space=pl.ANY)
    buf = shape(*BUF)
    mega = 1 << 20
    slots_a, slots_b = 3, 2
    outs = pl.pallas_call(
        first_kernel,
        out_shape=[shape(*gu_shape), buf] + [buf] * 9 + [shape(*gu_shape), buf] + [buf] * 36,
        in_specs=[smem] * 2 + [vmem] * 6 + [hbm] * 6,
        out_specs=[hbm] * 8 + [vmem] * 5 + [hbm] * 36,
        scratch_shapes=[pltpu.VMEM(BUF, BF)] * 18
        + [pltpu.VMEM(gu_shape, BF), pltpu.VMEM(BUF, BF)]
        + [pltpu.VMEM((ROWS, 1024), BF)] * 2
        + [pltpu.VMEM((ROWS, 512), BF), pltpu.VMEM((ROWS, 1024), BF)]
        + semaphores(6, slots_a)
        + bounce_buffers(slots_a),
        compiler_params=pltpu.CompilerParams(
            collective_id=0, has_side_effects=True, vmem_limit_bytes=62 * mega
        ),
    )(source, source_x, place, place_gate, there, back, tokens, cotangent, *arrays)
    home_gu, home_dn = outs[0], outs[1]
    m_pieces, q_pieces, y_pieces = outs[2:5], outs[5:8], outs[8:11]
    g_gu, g_dn = outs[11:13]

    outs = pl.pallas_call(
        second_kernel,
        out_shape=[shape(N, 1024)] + [shape(*gu_shape), buf] * 2 + [buf] * 24,
        in_specs=[smem] * 6 + [vmem] * 2 + [hbm] * 11,
        out_specs=[vmem] + [hbm] * 28,
        scratch_shapes=[pltpu.VMEM(BUF, BF)] * 18
        + [pltpu.VMEM((3, N, 16, 256), F32), pltpu.VMEM((ROWS, 1024), BF)]
        + semaphores(4, slots_b)
        + bounce_buffers(slots_b),
        compiler_params=pltpu.CompilerParams(
            collective_id=1, has_side_effects=True, vmem_limit_bytes=62 * mega
        ),
    )(
        source,
        source_x,
        order,
        order_x,
        last,
        keep,
        there,
        combine,
        g_gu,
        g_dn,
        *y_pieces,
        *m_pieces,
        *q_pieces,
    )
    layer_out, m_gu, m_dn, q_gu, q_dn = outs[:5]

    def step(w, m, q):
        return (
            w.astype(F32) - 0.01 * m.astype(F32) / (jnp.sqrt(q.astype(F32)) + 1e-8)
        ).astype(BF)

    up_shape, down_shape = (1, 1024, 1024), (1, 512, 1024)
    return (
        layer_out,
        step(home_gu, m_gu, q_gu).reshape(up_shape),
        step(home_dn, m_dn, q_dn).reshape(down_shape),
        m_gu.reshape(up_shape),
        m_dn.reshape(down_shape),
        q_gu.reshape(up_shape),
        q_dn.reshape(down_shape),
    )


def solution(mesh):
    tok = P("ep", None)
    slot = P("ep", None, None)
    return jax.shard_map(
        shards,
        mesh=mesh,
        in_specs=(tok,) * 4 + (P(), P()) + (slot,) * 6,
        out_specs=(tok,) + (slot,) * 6,
        check_vma=False,
    )
```

```python
import jax
import jax.numpy as jnp
import numpy as np
from jax import lax
from jax.sharding import PartitionSpec as P
from jax.experimental import pallas as pl
from jax.experimental.pallas import tpu as pltpu

N = 128
CAP = 12
ROWS = N * CAP
BF = jnp.bfloat16
F32 = jnp.float32
MESH = pl.DeviceIdType.MESH

ORDER = (("x", "y", "z"), ("y", "z", "x"), ("z", "x", "y"))
BUF = (4, 4, 2, 16, 1024)


def coordinates():
    me = lax.axis_index("ep")
    return {"z": me // 32, "y": (me // 8) % 4, "x": (me // 2) % 4, "c": me % 2}


def device(at, **moved):
    q = {**at, **moved}
    return (q["z"] * 32 + q["y"] * 8 + q["x"] * 2 + q["c"],)


def cut(ref, rows, **kw):
    if "x" in kw:
        cols = pl.ds(pl.multiple_of(kw["x"] * 256, 256), 256)
    else:
        cols = slice(None)
    every = slice(None)
    row = every if rows is None else pl.ds(rows, 16)
    return ref.at[kw.get("z", every), kw.get("y", every), kw.get("c", every), row, cols]


def bounce_shape(stream, phase):
    size = {"z": 4, "y": 4, "c": 2, "x": 4}
    size[ORDER[stream][phase]] = None
    if phase == 0:
        size["c"] = None
    lead = tuple(size[a] for a in "zyc" if size[a])
    return lead + (16, 1024 if size["x"] else 256)


def enter(at):
    bar = pltpu.get_barrier_semaphore()
    pl.semaphore_signal(bar, inc=1, device_id=device(at, c=1 - at["c"]), device_id_type=MESH)
    for axis in "zyx":
        for d in (1, 2, 3):
            for dc in (0, 1):
                there = {axis: (at[axis] + d) % 4, "c": (at["c"] + dc) % 2}
                pl.semaphore_signal(
                    bar, inc=1, device_id=device(at, **there), device_id_type=MESH
                )
    pl.semaphore_wait(bar, 19)


class Exchanges:
    def __init__(self, at, stages, sends, receives, bounces, bounce_sems):
        self.at, self.stages = at, stages
        self.sends, self.receives = sends, receives
        self.bounces, self.bounce_sems = bounces, bounce_sems
        self.slots = len(bounces) // 9
        self.held = {}
        self.drained = set()
        self.ids = {g: i for i, g in enumerate(stages)}

    def start(self, g, phase):
        at, i = self.at, self.ids[g]
        loads = []
        if phase:
            for s in range(3):
                self._arrived(g, s, phase - 1)
        for s in range(3):
            (src, src_rows), (dst, dst_rows) = self.stages[g][s][phase : phase + 2]
            axis = ORDER[s][phase]
            mine = {axis: at[axis]}
            if phase == 0:
                mine["c"] = at["c"]
            used = {v for k, v in self.held.items() if k[1:] == (s, phase)}
            slot = min(set(range(self.slots)) - used)
            self.held[g, s, phase] = slot
            n = slot * 9 + s * 3 + phase
            load = pltpu.make_async_copy(
                cut(src, src_rows, **mine), self.bounces[n], self.bounce_sems.at[n]
            )
            load.start()
            loads.append((load, n, cut(dst, dst_rows, **mine), s))
        for d in (2, 1, 3, 0):
            for dc in (0, 1) if phase == 0 else (0,):
                if d == 0 and dc == 0:
                    continue
                for s in range(3):
                    (src, src_rows), (dst, dst_rows) = self.stages[g][s][phase : phase + 2]
                    axis = ORDER[s][phase]
                    mine = {axis: at[axis]}
                    there = {axis: (at[axis] + d) % 4}
                    if phase == 0:
                        mine["c"] = at["c"]
                        there["c"] = (at["c"] + dc) % 2
                    pltpu.make_async_remote_copy(
                        cut(src, src_rows, **there),
                        cut(dst, dst_rows, **mine),
                        self.sends.at[i, s, phase],
                        self.receives.at[i, s, phase],
                        device_id=device(at, **there),
                        device_id_type=MESH,
                    ).start()
        for load, n, dst, s in loads:
            load.wait()
            pltpu.make_async_copy(
                self.bounces[n], dst, self.receives.at[i, s, phase]
            ).start()

    def _arrived(self, g, s, phase):
        dst, rows = self.stages[g][s][phase + 1]
        whole = cut(dst, rows)
        pltpu.make_async_copy(whole, whole, self.receives.at[self.ids[g], s, phase]).wait()
        del self.held[g, s, phase]

    def finish(self, g):
        for s in range(3):
            self._arrived(g, s, 2)

    def sent(self, g, phase):
        if (g, phase) in self.drained:
            return
        self.drained.add((g, phase))
        for s in range(3):
            ref, rows = self.stages[g][s][phase + 1]
            row = slice(None) if rows is None else pl.ds(rows, 16)
            part = ref.at[:, :, :, row, pl.ds(0, 768 if phase else 896)]
            pltpu.make_async_copy(part, part, self.sends.at[self.ids[g], s, phase]).wait()

    def drain(self):
        for g in self.ids:
            for phase in range(3):
                self.sent(g, phase)


def to_pieces(back, rows48, store):
    stacked = jnp.concatenate([rows48[:, q * 256 : q * 256 + 256] for q in range(4)], axis=0)
    moved = jnp.dot(back, stacked, preferred_element_type=F32).astype(BF)
    for s in range(3):
        store(s, moved[s * 64 : s * 64 + 64].reshape(4, 16, 256))


def from_pieces(there, refs, g, x):
    parts = [
        refs[s][g // 2, pl.ds(2 * (g % 2), 2), :, :, pl.ds(x * 256, 256)].reshape(64, 256)
        for s in range(3)
    ]
    return jnp.dot(
        there, jnp.concatenate(parts, axis=0), preferred_element_type=F32
    ).astype(BF)


def relayout(there, refs, out):
    def body(g, carry):
        for x in range(4):
            moved = from_pieces(there, refs, g, x)
            at = pl.multiple_of(x * 384 + g * 48, 16)
            for q in range(4):
                out[pl.ds(at, 48), q * 256 : q * 256 + 256] = moved[q * 48 : q * 48 + 48]
        return carry

    lax.fori_loop(0, 8, body, 0)


def piece_of(ref, table, j):
    full = ref[table[0, j], table[1, j], table[2, j]].astype(F32)
    return sum(full[:, x * 256 : x * 256 + 256] * table[3 + x, j].astype(F32) for x in range(4))


def routing(routes, gates, place, weighed):
    lane = lax.broadcasted_iota(jnp.int32, (N, N), 1)
    line = lax.broadcasted_iota(jnp.int32, (N, N), 0)
    slot = ((lane >> 3) & 3) * 32 + ((lane >> 1) & 3) * 8 + (lane >> 5) * 2 + (lane & 1)
    hit = jnp.zeros((N, N), F32)
    gate = jnp.zeros((N, N), F32)
    for k in range(8):
        named = routes[:, k : k + 1] == slot
        hit = jnp.where(named, 1.0, hit)
        gate = jnp.where(named, gates[:, k : k + 1], gate)
    below = jnp.where(line > lane, 1.0, 0.0).astype(BF)
    row = jnp.dot(below, hit.astype(BF), preferred_element_type=F32)
    row = jnp.where(hit > 0.0, row, -1.0).T
    gate = gate.T
    high = gate.astype(BF)
    rest = gate - high.astype(F32)
    middle = rest.astype(BF)
    low = (rest - middle.astype(F32)).astype(BF)
    row = row.astype(BF)

    def body(b, carry):
        i = lax.broadcasted_iota(jnp.int32, (192, N), 0)
        first = (lax.broadcasted_iota(jnp.int32, (192, N), 1) - b * 16) * CAP
        spread = jnp.where((i >= first) & (i < first + CAP), 1.0, 0.0).astype(BF)
        rank = i.astype(F32)
        rank = rank - jnp.floor((rank + 0.5) * (1.0 / CAP)) * CAP

        def copies(v):
            return jnp.dot(spread, v, preferred_element_type=F32)

        here = copies(row) == rank
        r = pl.ds(pl.multiple_of(b * 192, 16), 192)
        place[r] = jnp.where(here, 1.0, 0.0).astype(BF)
        weighed[r] = jnp.where(here, copies(high) + copies(middle) + copies(low), 0.0)
        return carry

    lax.fori_loop(0, 8, body, 0)


def step_kernel(*refs):
    table, there, back, routes, gates, tokens, cotangent = refs[:7]
    w_gu, w_dn, m_gu, m_dn, q_gu, q_dn = refs[7:13]
    layer_out, home_gu, home_dn = refs[13:16]
    new_m, new_q = refs[16:18], refs[18:20]
    m_far, q_far = refs[20:23], refs[23:26]
    mids = refs[26:86]
    scratch = refs[86:]
    w_land, x_land, c_land, g_land, y_land = (scratch[i : i + 3] for i in range(0, 15, 3))
    w_stage, x_send, c_send = (scratch[i : i + 3] for i in range(15, 24, 3))
    gu, dn, g_gu, g_dn, xs, cs, hidden, d_pre, sums, place, weighed = scratch[24:35]
    sends, receives, bounce_sems, copy_sem = scratch[35:39]
    bounces = scratch[39:]
    y_send, m_send, q_send = x_send, w_stage, c_send
    m_old, q_old, ys = x_land, c_land, xs

    def raw(a, b):
        return [(a, 0), (a, 16), (b, None)]

    def plain(group):
        return [(r, None) for r in group]

    ends = {
        "w": (raw(w_gu, w_dn), plain(w_land)),
        "x": (plain(x_send), plain(x_land)),
        "c": (plain(c_send), plain(c_land)),
        "home": (plain(w_stage), raw(gu, dn)),
        "m": (raw(m_gu, m_dn), plain(m_far)),
        "q": (raw(q_gu, q_dn), plain(q_far)),
        "g": (raw(g_gu, g_dn), plain(g_land)),
        "y": (plain(y_send), plain(y_land)),
        "new_m": (plain(m_send), raw(*new_m)),
        "new_q": (plain(q_send), raw(*new_q)),
    }
    stages = {}
    for i, (g, (first, end)) in enumerate(ends.items()):
        stages[g] = [
            (first[s], (mids[i * 6 + s], None), (mids[i * 6 + 3 + s], None), end[s])
            for s in range(3)
        ]
    at = coordinates()
    enter(at)
    ex = Exchanges(at, stages, sends, receives, bounces, bounce_sems)

    def pair(g):
        return pl.ds(2 * (g % 2), 2)

    def dispatch(rows, scaled, out):
        def body(g, carry):
            for x in range(4):
                r = pl.ds(pl.multiple_of(x * 384 + g * 48, 16), 48)
                got = jnp.dot(place[r], rows[...], preferred_element_type=F32)
                if scaled:
                    got = got * jnp.sum(weighed[r], axis=1, keepdims=True)

                def store(s, value, x=x):
                    out[s][g // 2, pair(g), :, :, x * 256 : x * 256 + 256] = value.reshape(
                        2, 2, 16, 256
                    )

                to_pieces(back[...], got.astype(BF), store)
            return carry

        lax.fori_loop(0, 8, body, 0)

    def each_slot(do):
        def body(i, carry):
            z, y, c = i // 8, (i // 2) % 4, i % 2
            for x in range(4):
                for s in range(3):
                    do(s, (z, y, c, slice(None), slice(x * 256, x * 256 + 256)), i * 4 + x)
            return carry

        lax.fori_loop(0, 32, body, 0)

    def forward(b, carry):
        r = pl.ds(pl.multiple_of(b * 192, 16), 192)
        pre = jnp.zeros((192, 1024), F32)
        for k in range(4):
            pre += jnp.dot(
                xs[r, k * 256 : k * 256 + 256],
                gu[k].reshape(256, 1024),
                preferred_element_type=F32,
            )
        gate, up = pre[:, :512], pre[:, 512:]
        d_hid = jnp.concatenate(
            [
                lax.dot_general(
                    cs[r],
                    dn[k].reshape(128, 1024),
                    (((1,), (1,)), ((), ())),
                    preferred_element_type=F32,
                )
                for k in range(4)
            ],
            axis=1,
        )
        sig = jax.nn.sigmoid(gate)
        act = gate * sig
        h = (act * up).astype(BF)
        hidden[r] = h
        d_pre[r, 0:512] = (d_hid * up * sig * (1.0 + gate * (1.0 - sig))).astype(BF)
        d_pre[r, 512:1024] = (d_hid * act).astype(BF)
        y = jnp.zeros((192, 1024), F32)
        for k in range(4):
            y += jnp.dot(
                h[:, k * 128 : k * 128 + 128],
                dn[k].reshape(128, 1024),
                preferred_element_type=F32,
            )
        y = y.astype(BF)
        cols = pl.ds(pl.multiple_of(b // 2 * 256, 256), 256)
        for j in range(4):
            g = b % 2 * 4 + j

            def store(s, value):
                y_send[s][g // 2, pair(j), :, :, cols] = value.reshape(2, 2, 16, 256)

            to_pieces(back[...], y[j * 48 : j * 48 + 48], store)
        return carry

    ex.start("w", 0)
    ex.start("m", 0)
    routing(routes, gates, place, weighed)
    dispatch(tokens, False, x_send)
    ex.start("w", 1)
    ex.start("x", 0)
    dispatch(cotangent, True, c_send)
    ex.start("w", 2)
    ex.start("c", 0)
    ex.start("x", 1)
    ex.start("m", 1)
    ex.finish("w")

    def select(s, here, j):
        w_stage[s][here] = piece_of(w_land[s], table, j).astype(BF)

    each_slot(select)
    ex.start("home", 0)
    ex.start("c", 1)
    ex.start("x", 2)
    ex.start("home", 1)
    ex.start("c", 2)
    ex.start("q", 0)
    ex.start("home", 2)
    ex.start("m", 2)
    ex.finish("x")
    relayout(there[...], x_land, xs)
    ex.finish("c")
    relayout(there[...], c_land, cs)
    ex.start("q", 1)
    ex.finish("home")
    keep_gu = pltpu.make_async_copy(gu, home_gu, copy_sem.at[0])
    keep_dn = pltpu.make_async_copy(dn, home_dn, copy_sem.at[1])
    keep_gu.start()
    keep_dn.start()
    ex.sent("x", 0)
    lax.fori_loop(0, 8, forward, 0)
    ex.start("q", 2)
    for k in range(4):
        got = lax.dot_general(
            xs[:, k * 256 : k * 256 + 256],
            d_pre[...],
            (((0,), (0,)), ((), ())),
            preferred_element_type=F32,
        )
        g_gu[k] = got.astype(BF).reshape(4, 2, 32, 1024)
        got = lax.dot_general(
            hidden[:, k * 128 : k * 128 + 128],
            cs[...],
            (((0,), (0,)), ((), ())),
            preferred_element_type=F32,
        )
        g_dn[k] = got.astype(BF).reshape(4, 2, 16, 1024)
    ex.start("g", 0)
    ex.start("y", 0)
    ex.finish("m")
    ex.finish("q")
    fetch = [
        pltpu.make_async_copy(a, b, copy_sem.at[2 + i])
        for i, (a, b) in enumerate(zip(m_far + q_far, m_old + q_old))
    ]
    for f in fetch:
        f.start()
    ex.start("g", 1)
    ex.start("y", 1)
    ex.start("g", 2)
    for s in range(3):
        sums[s, N] = jnp.zeros((16, 256), F32)
    ex.finish("g")

    def add(s, here, j):
        sums[s, j] = g_land[s][here].astype(F32) + sums[s, table[7, j]]

    each_slot(add)
    ex.start("y", 2)
    for f in fetch:
        f.wait()
    ex.sent("home", 0)
    ex.sent("c", 0)

    def update_first(s, here, j):
        was = piece_of(m_old[s], table, j)
        m_send[s][here] = (0.9 * was + 0.1 * sums[s, table[8, j]]).astype(BF)

    def update_second(s, here, j):
        was = piece_of(q_old[s], table, j)
        total = sums[s, table[8, j]]
        q_send[s][here] = (0.95 * was + 0.05 * total * total).astype(BF)

    each_slot(update_first)
    ex.start("new_m", 0)
    each_slot(update_second)
    ex.start("new_q", 0)
    ex.start("new_m", 1)
    ex.finish("y")
    relayout(there[...], y_land, ys)
    ex.start("new_q", 1)
    ex.start("new_m", 2)
    high = weighed[...].astype(BF)
    low = (weighed[...] - high.astype(F32)).astype(BF)
    over_rows = (((0,), (0,)), ((), ()))
    mixed = lax.dot_general(high, ys[...], over_rows, preferred_element_type=F32)
    mixed += lax.dot_general(low, ys[...], over_rows, preferred_element_type=F32)
    layer_out[...] = mixed.astype(BF)
    ex.start("new_q", 2)
    ex.finish("new_m")
    ex.finish("new_q")
    ex.drain()
    keep_gu.wait()
    keep_dn.wait()


def weights_kernel(*refs):
    for i in range(2):
        w, m, q = (refs[3 * i + k] for k in range(3))
        new_w, new_m, new_q = (refs[6 + 3 * i + k] for k in range(3))
        rows = new_w.shape[1]
        first, second = m[...].reshape(rows, 1024), q[...].reshape(rows, 1024)
        weight = w[...].reshape(rows, 1024).astype(F32)
        change = 0.01 * first.astype(F32) / (jnp.sqrt(second.astype(F32)) + 1e-8)
        new_w[0] = (weight - change).astype(BF)
        new_m[0] = first
        new_q[0] = second


def shape(*dims, dtype=BF):
    return jax.ShapeDtypeStruct(dims, dtype)


def semaphores(groups, slots):
    dma = pltpu.SemaphoreType.DMA
    return [dma((groups, 3, 3)), dma((groups, 3, 3)), dma((slots * 9,)), dma((8,))]


def bounce_buffers(slots):
    return [
        pltpu.VMEM(bounce_shape(s, phase), BF)
        for _ in range(slots)
        for s in range(3)
        for phase in range(3)
    ]


def orders():
    i = np.arange(192)
    flat = i // 64 * 16 + i % 16
    where_to = flat // 12 * 48 + (i % 64) // 16 * 12 + flat % 12
    there = (i[:, None] == where_to[None, :]).astype(np.float32)
    return jnp.asarray(there, BF), jnp.asarray(there.T, BF)


def tables(old_experts, source):
    j = jnp.arange(N, dtype=jnp.int32)
    src = source.reshape(4, 4, 4, 2).transpose(0, 1, 3, 2).reshape(N)
    expert = jnp.sum(jnp.where(src[:, None] == j[None, :], old_experts[None, :], 0), axis=1)
    same = expert[:, None] == expert[None, :]
    before = jnp.max(jnp.where(same & (j[None, :] < j[:, None]), j[None, :], -1), axis=1)
    before = jnp.where(before < 0, N, before)
    last = jnp.max(jnp.where(same, j[None, :], -1), axis=1)
    x = (src // 2) % 4
    rows = [src // 32, (src // 8) % 4, src % 2] + [(x == k).astype(jnp.int32) for k in range(4)]
    return jnp.stack(rows + [before, last])


def shards(
    tokens,
    cotangent,
    routes,
    gate_weights,
    old_experts,
    source,
    gate_up_weight,
    down_weight,
    first_gate_up,
    first_down,
    second_gate_up,
    second_down,
):
    table = tables(old_experts, source)
    there, back = orders()
    gu_shape, dn_shape = (4, 4, 2, 32, 1024), BUF
    arrays = (
        gate_up_weight.reshape(gu_shape),
        down_weight.reshape(dn_shape),
        first_gate_up.reshape(gu_shape),
        first_down.reshape(dn_shape),
        second_gate_up.reshape(gu_shape),
        second_down.reshape(dn_shape),
    )
    smem = pl.BlockSpec(memory_space=pltpu.SMEM)
    vmem = pl.BlockSpec(memory_space=pltpu.VMEM)
    hbm = pl.BlockSpec(memory_space=pl.ANY)
    gu, buf = shape(*gu_shape), shape(*BUF)
    mega = 1 << 20
    slots = 4
    outs = pl.pallas_call(
        step_kernel,
        out_shape=[shape(N, 1024)] + [gu, buf] * 3 + [buf] * 66,
        in_specs=[smem] + [vmem] * 6 + [hbm] * 6,
        out_specs=[vmem] + [hbm] * 72,
        scratch_shapes=[pltpu.VMEM(BUF, BF)] * 24
        + [pltpu.VMEM(gu_shape, BF), pltpu.VMEM(BUF, BF)] * 2
        + [pltpu.VMEM((ROWS, 1024), BF)] * 2
        + [pltpu.VMEM((ROWS, 512), BF), pltpu.VMEM((ROWS, 1024), BF)]
        + [pltpu.VMEM((3, N + 1, 16, 256), F32)]
        + [pltpu.VMEM((ROWS, N), BF), pltpu.VMEM((ROWS, N), F32)]
        + semaphores(10, slots)
        + bounce_buffers(slots),
        compiler_params=pltpu.CompilerParams(
            collective_id=0, has_side_effects=True, vmem_limit_bytes=63 * mega
        ),
    )(table, there, back, routes, gate_weights, tokens, cotangent, *arrays)
    layer_out, home_gu, home_dn, m_gu, m_dn, q_gu, q_dn = outs[:7]

    def pieces(rows):
        return pl.BlockSpec((1, 2, 2, rows, 1024), lambda i: (i // 2, i % 2, 0, 0, 0))

    def whole(rows):
        return pl.BlockSpec((1, rows, 1024), lambda i: (0, i, 0))

    new = pl.pallas_call(
        weights_kernel,
        grid=(8,),
        out_shape=[shape(1, 1024, 1024)] * 3 + [shape(1, 512, 1024)] * 3,
        in_specs=[pieces(32)] * 3 + [pieces(16)] * 3,
        out_specs=[whole(128)] * 3 + [whole(64)] * 3,
        compiler_params=pltpu.CompilerParams(vmem_limit_bytes=32 * mega),
    )(home_gu, m_gu, q_gu, home_dn, m_dn, q_dn)
    return layer_out, new[0], new[3], new[1], new[4], new[2], new[5]


def solution(mesh):
    tok = P("ep", None)
    slot = P("ep", None, None)
    return jax.shard_map(
        shards,
        mesh=mesh,
        in_specs=(tok,) * 4 + (P(), P()) + (slot,) * 6,
        out_specs=(tok,) + (slot,) * 6,
        check_vma=False,
    )
```

```python
import jax
import jax.numpy as jnp
import numpy as np
from jax import lax
from jax.sharding import PartitionSpec as P
from jax.experimental import pallas as pl
from jax.experimental.pallas import tpu as pltpu

N = 128
CAP = 12
ROWS = N * CAP
BF = jnp.bfloat16
F32 = jnp.float32
MESH = pl.DeviceIdType.MESH

ORDER = (("x", "y", "z"), ("y", "z", "x"), ("z", "x", "y"))
BUF = (4, 4, 2, 16, 1024)
SLOTS = (2, 3, 2)

X_WIDE = (384, 384, 256)
C_WIDE = (384, 256, 384)
Y_WIDE = (256, 384, 384)
STEP = {"z": 32, "y": 8, "x": 2}


def coordinates():
    me = lax.axis_index("ep")
    return {"z": me // 32, "y": (me // 8) % 4, "x": (me // 2) % 4, "c": me % 2}


def device(at, **moved):
    q = {**at, **moved}
    return (q["z"] * 32 + q["y"] * 8 + q["x"] * 2 + q["c"],)


def cut(ref, rows, **kw):
    if "x" in kw:
        cols = pl.ds(pl.multiple_of(kw["x"] * 256, 256), 256)
    else:
        cols = slice(None)
    every = slice(None)
    row = every if rows is None else pl.ds(rows, 16)
    return ref.at[kw.get("z", every), kw.get("y", every), kw.get("c", every), row, cols]


def bounce_shape(stream, phase):
    size = {"z": 4, "y": 4, "c": 2, "x": 4}
    size[ORDER[stream][phase]] = None
    if phase == 0:
        size["c"] = None
    lead = tuple(size[a] for a in "zyc" if size[a])
    return lead + (16, 1024 if size["x"] else 256)


def enter(at):
    bar = pltpu.get_barrier_semaphore()
    pl.semaphore_signal(bar, inc=1, device_id=device(at, c=1 - at["c"]), device_id_type=MESH)
    for axis in "zyx":
        for d in (1, 2, 3):
            for dc in (0, 1):
                there = {axis: (at[axis] + d) % 4, "c": (at["c"] + dc) % 2}
                pl.semaphore_signal(
                    bar, inc=1, device_id=device(at, **there), device_id_type=MESH
                )
    pl.semaphore_wait(bar, 19)


class Exchanges:
    def __init__(self, at, stages, near, sends, receives, bounces, bounce_sems):
        self.at, self.stages, self.near = at, stages, near
        self.sends, self.receives = sends, receives
        self.bounces, self.bounce_sems = bounces, bounce_sems
        self.held = {}
        self.drained = set()
        self.ids = {g: i for i, g in enumerate(stages)}

    def start(self, g, phase):
        at, i = self.at, self.ids[g]
        loads = []
        if phase:
            for s in range(3):
                self._arrived(g, s, phase - 1)
        for s in range(3):
            (src, src_rows), (dst, dst_rows) = self.stages[g][s][phase : phase + 2]
            axis = ORDER[s][phase]
            mine = {axis: at[axis]}
            if phase == 0:
                mine["c"] = at["c"]
            if (g, phase) in self.near:
                pltpu.make_async_copy(
                    cut(src, src_rows, **mine),
                    cut(dst, dst_rows, **mine),
                    self.receives.at[i, s, phase],
                ).start()
                continue
            used = {v for k, v in self.held.items() if k[1:] == (s, phase)}
            slot = min(set(range(SLOTS[phase])) - used)
            self.held[g, s, phase] = slot
            n = sum(SLOTS[:phase]) * 3 + slot * 3 + s
            load = pltpu.make_async_copy(
                cut(src, src_rows, **mine), self.bounces[n], self.bounce_sems.at[n]
            )
            load.start()
            loads.append((load, n, cut(dst, dst_rows, **mine), s))
        for d in (2, 1, 3, 0):
            for dc in (0, 1) if phase == 0 else (0,):
                if d == 0 and dc == 0:
                    continue
                for s in range(3):
                    (src, src_rows), (dst, dst_rows) = self.stages[g][s][phase : phase + 2]
                    axis = ORDER[s][phase]
                    mine = {axis: at[axis]}
                    there = {axis: (at[axis] + d) % 4}
                    if phase == 0:
                        mine["c"] = at["c"]
                        there["c"] = (at["c"] + dc) % 2
                    pltpu.make_async_remote_copy(
                        cut(src, src_rows, **there),
                        cut(dst, dst_rows, **mine),
                        self.sends.at[i, s, phase],
                        self.receives.at[i, s, phase],
                        device_id=device(at, **there),
                        device_id_type=MESH,
                    ).start()
        for load, n, dst, s in loads:
            load.wait()
            pltpu.make_async_copy(
                self.bounces[n], dst, self.receives.at[i, s, phase]
            ).start()

    def _arrived(self, g, s, phase):
        dst, rows = self.stages[g][s][phase + 1]
        whole = cut(dst, rows)
        pltpu.make_async_copy(whole, whole, self.receives.at[self.ids[g], s, phase]).wait()
        self.held.pop((g, s, phase), None)

    def finish(self, g):
        for s in range(3):
            self._arrived(g, s, 2)

    def sent(self, g, phase):
        if (g, phase) in self.drained:
            return
        self.drained.add((g, phase))
        for s in range(3):
            ref, rows = self.stages[g][s][phase + 1]
            row = slice(None) if rows is None else pl.ds(rows, 16)
            part = ref.at[:, :, :, row, pl.ds(0, 768 if phase else 896)]
            pltpu.make_async_copy(part, part, self.sends.at[self.ids[g], s, phase]).wait()

    def drain(self):
        for g in self.ids:
            for phase in range(3):
                self.sent(g, phase)


def spans(wide):
    return [(sum(wide[:s]), wide[s]) for s in range(3)]


class TokenExchanges:
    def __init__(self, at, sends, receives):
        self.at, self.sends, self.receives = at, sends, receives

    def _remote(self, src, dst, there, key, extra=0):
        pltpu.make_async_remote_copy(
            src,
            dst,
            self.sends.at[(*key, extra)],
            self.receives.at[key],
            device_id=device(self.at, **there),
            device_id_type=MESH,
        ).start()

    def ring(self, g, phase, s, pairs, key=None):
        axis = ORDER[s][0]
        for d in (2, 1, 3):
            there = (self.at[axis] + d) % 4
            src, dst = pairs(there)
            self._remote(src, dst, {axis: there}, key or (g, s, phase))

    def second(self, g, phase, src, dst):
        at = self.at
        for d in (2, 1, 3, 0):
            for dc in (0, 1):
                for s in range(3):
                    axis = ORDER[s][1]
                    there = {axis: (at[axis] + d) % 4, "c": (at["c"] + dc) % 2}
                    here = dst[s].at[at[axis], at["c"]]
                    if d == 0 and dc == 0:
                        pltpu.make_async_copy(
                            src[s].at[at[axis], at["c"]], here, self.receives.at[g, s, phase]
                        ).start()
                    else:
                        part = src[s].at[there[axis], there["c"]]
                        self._remote(part, here, there, (g, s, phase), dc)

    def third(self, g, phase, src, dst):
        at = self.at
        for d in (2, 1, 3, 0):
            for s in range(3):
                axis = ORDER[s][2]
                to = (at[axis] + d) % 4
                here = dst[s].at[:, :, at[axis]]
                if d == 0:
                    pltpu.make_async_copy(
                        src[s].at[:, :, to], here, self.receives.at[g, s, phase]
                    ).start()
                else:
                    self._remote(src[s].at[:, :, to], here, {axis: to}, (g, s, phase))

    def arrived(self, g, phase, s, ref):
        pltpu.make_async_copy(ref, ref, self.receives.at[g, s, phase]).wait()

    def left(self, g, phase, s, ref, extra=0):
        pltpu.make_async_copy(ref, ref, self.sends.at[g, s, phase, extra]).wait()


def arrange(swap, land, wide, out):
    def body(g, carry):
        c = g % 2
        for s, (start, n) in enumerate(spans(wide)):
            cols = slice(start, start + n)
            if s == 0:
                out[pl.ds(pl.multiple_of(g * 192, 16), 192), cols] = land[s][g // 2, c].reshape(192, n)
            elif s == 1:
                rows = land[s][g // 2, c].reshape(192, n)
                rows = jnp.dot(swap, rows, preferred_element_type=F32).astype(BF)
                for y in range(4):
                    r = pl.multiple_of(((y * 2 + c) * 4 + g // 2) * 48, 16)
                    out[pl.ds(r, 48), cols] = rows[y * 48 : y * 48 + 48]
            else:
                rows = jnp.concatenate([land[s][x, c, g // 2] for x in range(4)], axis=0)
                rows = jnp.dot(swap, rows, preferred_element_type=F32).astype(BF)
                out[pl.ds(pl.multiple_of(g * 192, 16), 192), cols] = rows
        return carry

    lax.fori_loop(0, 8, body, 0)


def piece_of(ref, table, j):
    full = ref[table[0, j], table[1, j], table[2, j]].astype(F32)
    return sum(full[:, x * 256 : x * 256 + 256] * table[3 + x, j].astype(F32) for x in range(4))


def routing(at, s, routes, gates, ranks, weights):
    lane = lax.broadcasted_iota(jnp.int32, (N, N), 1)
    line = lax.broadcasted_iota(jnp.int32, (N, N), 0)
    first, second, third = ORDER[s]
    slot = (line >> 5) * STEP[second] + ((line >> 4) & 1) + (line & 3) * STEP[third]
    slot = slot + at[first] * STEP[first]
    block = (line >> 2) & 3
    hit = jnp.zeros((N, N), F32)
    gate = jnp.zeros((N, N), F32)
    for b in range(4):
        wanted = jnp.where(block == b, slot, -1)
        for k in range(8):
            named = routes[b, k : k + 1, :] == wanted
            hit = jnp.where(named, 1.0, hit)
            gate = jnp.where(named, gates[b, k : k + 1, :], gate)
    above = jnp.where(line < lane, 1.0, 0.0).astype(BF)
    row = jnp.dot(hit.astype(BF), above, preferred_element_type=F32)
    ranks[...] = jnp.where(hit > 0.0, row + 1.0, 0.0).astype(BF)
    for part in range(3):
        high = gate.astype(BF)
        weights[part] = high
        gate = gate - high.astype(F32)


def placed(pick, ranks, g):
    lines = pl.ds(pl.multiple_of(g * 16, 16), 16)
    got = jnp.dot(pick, ranks[lines], preferred_element_type=F32)
    i = lax.broadcasted_iota(jnp.int32, (192, N), 0).astype(F32)
    rank = i - jnp.floor((i + 0.5) * (1.0 / CAP)) * CAP + 1.0
    return [got[k * 192 : k * 192 + 192] == rank for k in range(4)]


def weighed(pick, weights, here, g):
    lines = pl.ds(pl.multiple_of(g * 16, 16), 16)
    got = sum(
        jnp.dot(pick, weights[part, lines], preferred_element_type=F32) for part in range(3)
    )
    return jnp.concatenate(
        [jnp.where(here[k], got[k * 192 : k * 192 + 192], 0.0) for k in range(4)], axis=1
    )


def step_kernel(*refs):
    table, swap, pick, routes, gates, tokens, cotangent = refs[:7]
    w_gu, w_dn, m_gu, m_dn, q_gu, q_dn = refs[7:13]
    layer_out, home_gu, home_dn = refs[13:16]
    new_m, new_q = refs[16:18], refs[18:20]
    m_far, q_far = refs[20:23], refs[23:26]
    mids = refs[26:68]
    x_mid, c_mid, y_mid = refs[68:71], refs[71:74], refs[74:77]
    scratch = refs[77:]
    w_land, g_land, w_stage, old = (scratch[i : i + 3] for i in range(0, 12, 3))
    x_send, c_send, x_land, c_land, y_land = (scratch[i : i + 3] for i in range(12, 27, 3))
    x_all, c_all, y_parts = (scratch[i : i + 3] for i in range(27, 36, 3))
    gu, dn, g_gu, g_dn, xs, cs, hidden, d_pre, sums = scratch[36:45]
    all_routes, all_gates, ranks, weights, total, own = scratch[45:51]
    sends, receives, bounce_sems, copy_sem, t_sends, t_receives = scratch[51:57]
    bounces = scratch[57:]
    m_send, q_send = w_stage, w_land
    y_send = (x_send[2], x_send[0], x_send[1])
    my_parts = (x_all[2], x_all[0], x_all[1])
    y_kept = x_land[0]

    def raw(a, b):
        return [(a, 0), (a, 16), (b, None)]

    def plain(group):
        return [(r, None) for r in group]

    ends = {
        "w": (raw(w_gu, w_dn), plain(w_land)),
        "home": (plain(w_stage), raw(gu, dn)),
        "m": (raw(m_gu, m_dn), plain(m_far)),
        "q": (raw(q_gu, q_dn), plain(q_far)),
        "g": (raw(g_gu, g_dn), plain(g_land)),
        "new_m": (plain(m_send), raw(*new_m)),
        "new_q": (plain(q_send), raw(*new_q)),
    }
    stages = {}
    for i, (g, (first, end)) in enumerate(ends.items()):
        stages[g] = [
            (first[s], (mids[i * 6 + s], None), (mids[i * 6 + 3 + s], None), end[s])
            for s in range(3)
        ]
    at = coordinates()
    enter(at)
    near = {("w", 2), ("home", 0), ("home", 2), ("g", 0), ("g", 2), ("new_m", 0), ("new_q", 0)}
    ex = Exchanges(at, stages, near, sends, receives, bounces, bounce_sems)
    tx = TokenExchanges(at, t_sends, t_receives)

    def gather(g, rows, everyone, wide):
        for s, (start, n) in enumerate(spans(wide)):
            here = everyone[s].at[at[ORDER[s][0]]]
            mine = rows.at[:, pl.ds(start, n)]
            tx.ring(g, 0, s, lambda there, mine=mine, here=here: (mine, here))

    def keep_own(rows, everyone, wide):
        for s, (start, n) in enumerate(spans(wide)):
            everyone[s][at[ORDER[s][0]]] = rows[:, start : start + n]

    def gather_tables():
        for s in range(3):
            me = at[ORDER[s][0]]
            for k, (mine, everyone) in enumerate(((routes, all_routes), (gates, all_gates))):
                here = everyone.at[s, me]
                tx.ring(0, 0, s, lambda there, mine=mine, here=here: (mine, here), (3, s, k))
                everyone[s, me] = mine[...]

    def dispatch(s):
        def body(g, carry):
            here = placed(pick[...], ranks.at[s], g)
            place = jnp.concatenate(
                [jnp.where(h, 1.0, 0.0).astype(BF) for h in here], axis=1
            )
            gate = jnp.sum(weighed(pick[...], weights.at[s], here, g), axis=1, keepdims=True)
            for everyone, out, wide, factor in (
                (x_all, x_send, X_WIDE, None),
                (c_all, c_send, C_WIDE, gate),
            ):
                rows = everyone[s][...].reshape(512, wide[s])
                got = jnp.dot(place, rows, preferred_element_type=F32)
                if factor is not None:
                    got = got * factor
                out[s][g // 2, g % 2] = got.astype(BF).reshape(4, 48, wide[s])
            return carry

        lax.fori_loop(0, 8, body, 0)

    def combine(s):
        n = Y_WIDE[s]
        total[...] = jnp.zeros_like(total)
        over_rows = (((0,), (0,)), ((), ()))

        def body(g, carry):
            here = placed(pick[...], ranks.at[s], g)
            weight = weighed(pick[...], weights.at[s], here, g)
            high = weight.astype(BF)
            low = (weight - high.astype(F32)).astype(BF)
            rows = y_land[s][g // 2, g % 2].reshape(192, n)
            got = lax.dot_general(high, rows, over_rows, preferred_element_type=F32)
            got += lax.dot_general(low, rows, over_rows, preferred_element_type=F32)
            total[:, 0:n] += got
            return carry

        lax.fori_loop(0, 8, body, 0)
        start = spans(Y_WIDE)[s][0]
        for k in range(4):
            my_parts[s][k] = total[k * 128 : k * 128 + 128, 0:n].astype(BF)
        me = at[ORDER[s][0]]
        own[:, start : start + n] = total[pl.ds(pl.multiple_of(me * 128, 128), 128), 0:n]
        tx.ring(2, 2, s, lambda there: (my_parts[s].at[there], y_parts[s].at[me]))

    def each_slot(do):
        def body(i, carry):
            z, y, c = i // 8, (i // 2) % 4, i % 2
            for x in range(4):
                for s in range(3):
                    do(s, (z, y, c, slice(None), slice(x * 256, x * 256 + 256)), i * 4 + x)
            return carry

        lax.fori_loop(0, 32, body, 0)

    def forward(b, carry):
        r = pl.ds(pl.multiple_of(b * 192, 16), 192)
        pre = jnp.zeros((192, 1024), F32)
        for k in range(4):
            pre += jnp.dot(
                xs[r, k * 256 : k * 256 + 256],
                gu[k].reshape(256, 1024),
                preferred_element_type=F32,
            )
        gate, up = pre[:, :512], pre[:, 512:]
        d_hid = jnp.concatenate(
            [
                lax.dot_general(
                    cs[r],
                    dn[k].reshape(128, 1024),
                    (((1,), (1,)), ((), ())),
                    preferred_element_type=F32,
                )
                for k in range(4)
            ],
            axis=1,
        )
        sig = jax.nn.sigmoid(gate)
        act = gate * sig
        h = (act * up).astype(BF)
        hidden[r] = h
        d_pre[r, 0:512] = (d_hid * up * sig * (1.0 + gate * (1.0 - sig))).astype(BF)
        d_pre[r, 512:1024] = (d_hid * act).astype(BF)
        y = jnp.zeros((192, 1024), F32)
        for k in range(4):
            y += jnp.dot(
                h[:, k * 128 : k * 128 + 128],
                dn[k].reshape(128, 1024),
                preferred_element_type=F32,
            )
        y = y.astype(BF)
        (a0, an), (b0, bn), (c0, cn) = spans(Y_WIDE)
        y_send[0][b // 2, b % 2] = y[:, a0 : a0 + an].reshape(4, 48, an)
        y_kept[b // 2, b % 2] = y[:, b0 : b0 + bn].reshape(4, 48, bn)
        rows = jnp.dot(swap[...], y[:, c0 : c0 + cn], preferred_element_type=F32).astype(BF)
        for x in range(4):
            y_send[2][x, b % 2, b // 2] = rows[x * 48 : x * 48 + 48]
        return carry

    def turn(g, carry):
        rows = jnp.concatenate([y_kept[y, g % 2, g // 2] for y in range(4)], axis=0)
        rows = jnp.dot(swap[...], rows, preferred_element_type=F32).astype(BF)
        y_send[1][g // 2, g % 2] = rows.reshape(4, 48, Y_WIDE[1])
        return carry

    def tokens_arrived(g, phase, refs):
        for s in range(3):
            tx.arrived(g, phase, s, refs[s])

    def three(refs):
        return [r.at[pl.ds(0, 3)] for r in refs]

    gather_tables()
    gather(0, tokens, x_all, X_WIDE)
    gather(1, cotangent, c_all, C_WIDE)
    ex.start("w", 0)
    ex.start("m", 0)
    keep_own(tokens, x_all, X_WIDE)
    keep_own(cotangent, c_all, C_WIDE)
    for s in range(3):
        tx.arrived(3, 0, s, all_routes.at[s, pl.ds(0, 3)])
        tx.arrived(3, 1, s, all_gates.at[s, pl.ds(0, 3)])
        routing(at, s, all_routes.at[s], all_gates.at[s], ranks.at[s], weights.at[s])
    tokens_arrived(0, 0, three(x_all))
    tokens_arrived(1, 0, three(c_all))
    dispatch(0)
    ex.start("w", 1)
    dispatch(1)
    dispatch(2)
    tx.second(0, 1, x_send, x_mid)
    ex.start("w", 2)
    tx.second(1, 1, c_send, c_mid)
    ex.start("m", 1)
    ex.finish("w")

    def select(s, here, j):
        w_stage[s][here] = piece_of(w_land[s], table, j).astype(BF)

    each_slot(select)
    ex.start("home", 0)
    tokens_arrived(0, 1, x_mid)
    tx.third(0, 2, x_mid, x_land)
    ex.start("home", 1)
    tokens_arrived(1, 1, c_mid)
    tx.third(1, 2, c_mid, c_land)
    ex.start("home", 2)
    ex.start("m", 2)
    ex.start("q", 0)
    tokens_arrived(0, 2, x_land)
    arrange(swap[...], x_land, X_WIDE, xs)
    tokens_arrived(1, 2, c_land)
    arrange(swap[...], c_land, C_WIDE, cs)
    ex.finish("home")
    ex.start("q", 1)
    keep_gu = pltpu.make_async_copy(gu, home_gu, copy_sem.at[0])
    keep_dn = pltpu.make_async_copy(dn, home_dn, copy_sem.at[1])
    keep_gu.start()
    keep_dn.start()
    for s in range(3):
        tx.left(0, 1, s, x_mid[s].at[pl.ds(0, 3), 0], 0)
        tx.left(0, 1, s, x_mid[s].at[:, 0], 1)
    lax.fori_loop(0, 8, forward, 0)
    lax.fori_loop(0, 8, turn, 0)
    ex.start("q", 2)
    for k in range(4):
        got = lax.dot_general(
            xs[:, k * 256 : k * 256 + 256],
            d_pre[...],
            (((0,), (0,)), ((), ())),
            preferred_element_type=F32,
        )
        g_gu[k] = got.astype(BF).reshape(4, 2, 32, 1024)
        got = lax.dot_general(
            hidden[:, k * 128 : k * 128 + 128],
            cs[...],
            (((0,), (0,)), ((), ())),
            preferred_element_type=F32,
        )
        g_dn[k] = got.astype(BF).reshape(4, 2, 16, 1024)
    ex.start("g", 0)
    tx.third(2, 0, y_send, y_mid)
    ex.finish("m")
    ex.finish("q")

    def fetch(far, first):
        copies = [
            pltpu.make_async_copy(a, b, copy_sem.at[first + i])
            for i, (a, b) in enumerate(zip(far, old))
        ]
        for f in copies:
            f.start()
        return copies

    coming = fetch(m_far, 2)
    ex.start("g", 1)
    tokens_arrived(2, 0, y_mid)
    tx.second(2, 1, y_mid, y_land)
    ex.start("g", 2)
    for s in range(3):
        sums[s, N] = jnp.zeros((16, 256), F32)
        tx.left(0, 0, s, x_all[s].at[pl.ds(0, 3)])
    ex.finish("g")

    def add(s, here, j):
        sums[s, j] = g_land[s][here].astype(F32) + sums[s, table[7, j]]

    each_slot(add)
    for f in coming:
        f.wait()
    ex.sent("home", 0)

    def update_first(s, here, j):
        was = piece_of(old[s], table, j)
        m_send[s][here] = (0.9 * was + 0.1 * sums[s, table[8, j]]).astype(BF)

    def update_second(s, here, j):
        was = piece_of(old[s], table, j)
        total = sums[s, table[8, j]]
        q_send[s][here] = (0.95 * was + 0.05 * total * total).astype(BF)

    each_slot(update_first)
    ex.start("new_m", 0)
    for f in fetch(q_far, 5):
        f.wait()
    each_slot(update_second)
    ex.start("new_q", 0)
    tokens_arrived(2, 1, y_land)
    combine(0)
    ex.start("new_m", 1)
    combine(1)
    ex.start("new_q", 1)
    combine(2)
    ex.start("new_m", 2)
    for s, (start, n) in enumerate(spans(Y_WIDE)):
        tx.arrived(2, 2, s, y_parts[s].at[pl.ds(0, 3)])
        me = at[ORDER[s][0]]
        result = own[:, start : start + n]
        for d in (1, 2, 3):
            result += y_parts[s][(me + d) % 4].astype(F32)
        layer_out[:, start : start + n] = result.astype(BF)
    ex.start("new_q", 2)
    for s in range(3):
        tx.left(1, 0, s, c_all[s].at[pl.ds(0, 3)])
        tx.left(3, 0, s, all_routes.at[s, pl.ds(0, 3)])
        tx.left(3, 1, s, all_gates.at[s, pl.ds(0, 3)])
        tx.left(0, 2, s, x_mid[s].at[:, :, pl.ds(0, 3)])
        tx.left(1, 1, s, c_mid[s].at[pl.ds(0, 3), 0], 0)
        tx.left(1, 1, s, c_mid[s].at[:, 0], 1)
        tx.left(1, 2, s, c_mid[s].at[:, :, pl.ds(0, 3)])
        tx.left(2, 0, s, y_mid[s].at[:, :, pl.ds(0, 3)])
        tx.left(2, 1, s, y_mid[s].at[pl.ds(0, 3), 0], 0)
        tx.left(2, 1, s, y_mid[s].at[:, 0], 1)
        tx.left(2, 2, s, y_parts[s].at[pl.ds(0, 3)])
    ex.finish("new_m")
    ex.finish("new_q")
    ex.drain()
    keep_gu.wait()
    keep_dn.wait()


def weights_kernel(*refs):
    for i in range(2):
        w, m, q = (refs[3 * i + k] for k in range(3))
        new_w, new_m, new_q = (refs[6 + 3 * i + k] for k in range(3))
        rows = new_w.shape[1]
        first, second = m[...].reshape(rows, 1024), q[...].reshape(rows, 1024)
        weight = w[...].reshape(rows, 1024).astype(F32)
        change = 0.01 * first.astype(F32) / (jnp.sqrt(second.astype(F32)) + 1e-8)
        new_w[0] = (weight - change).astype(BF)
        new_m[0] = first
        new_q[0] = second


def shape(*dims, dtype=BF):
    return jax.ShapeDtypeStruct(dims, dtype)


def semaphores(groups):
    dma = pltpu.SemaphoreType.DMA
    return [
        dma((groups, 3, 3)),
        dma((groups, 3, 3)),
        dma((sum(SLOTS) * 3,)),
        dma((8,)),
        dma((4, 3, 3, 2)),
        dma((4, 3, 3)),
    ]


def bounce_buffers():
    return [
        pltpu.VMEM(bounce_shape(s, phase), BF)
        for phase in range(3)
        for _ in range(SLOTS[phase])
        for s in range(3)
    ]


def token_buffers(wide):
    return [(4, 2, 4, 48, n) for n in wide]


def constants():
    i = np.arange(192)
    swap = (i // 12 % 4 * 48 + i // 48 * 12 + i % 12)[:, None] == i[None, :]
    block = np.arange(4)[:, None, None]
    line = np.arange(16)[None, None, :]
    rows = i[None, :, None]
    pick = (rows // 12 % 4 == block) & (line // 4 == block) & (line % 4 == rows // 48)
    return (
        jnp.asarray(swap.astype(np.float32), BF),
        jnp.asarray(pick.reshape(768, 16).astype(np.float32), BF),
    )


def tables(old_experts, source):
    j = jnp.arange(N, dtype=jnp.int32)
    src = source.reshape(4, 4, 4, 2).transpose(0, 1, 3, 2).reshape(N)
    expert = jnp.sum(jnp.where(src[:, None] == j[None, :], old_experts[None, :], 0), axis=1)
    same = expert[:, None] == expert[None, :]
    before = jnp.max(jnp.where(same & (j[None, :] < j[:, None]), j[None, :], -1), axis=1)
    before = jnp.where(before < 0, N, before)
    last = jnp.max(jnp.where(same, j[None, :], -1), axis=1)
    x = (src // 2) % 4
    rows = [src // 32, (src // 8) % 4, src % 2] + [(x == k).astype(jnp.int32) for k in range(4)]
    return jnp.stack(rows + [before, last])


def shards(
    tokens,
    cotangent,
    routes,
    gate_weights,
    old_experts,
    source,
    gate_up_weight,
    down_weight,
    first_gate_up,
    first_down,
    second_gate_up,
    second_down,
):
    table = tables(old_experts, source)
    swap, pick = constants()
    gu_shape, dn_shape = (4, 4, 2, 32, 1024), BUF
    arrays = (
        gate_up_weight.reshape(gu_shape),
        down_weight.reshape(dn_shape),
        first_gate_up.reshape(gu_shape),
        first_down.reshape(dn_shape),
        second_gate_up.reshape(gu_shape),
        second_down.reshape(dn_shape),
    )
    smem = pl.BlockSpec(memory_space=pltpu.SMEM)
    vmem = pl.BlockSpec(memory_space=pltpu.VMEM)
    hbm = pl.BlockSpec(memory_space=pl.ANY)
    gu, buf = shape(*gu_shape), shape(*BUF)
    mega = 1 << 20
    outs = pl.pallas_call(
        step_kernel,
        out_shape=[shape(N, 1024)]
        + [gu, buf] * 3
        + [buf] * 48
        + [shape(*b) for wide in (X_WIDE, C_WIDE, Y_WIDE) for b in token_buffers(wide)],
        in_specs=[smem] + [vmem] * 6 + [hbm] * 6,
        out_specs=[vmem] + [hbm] * 63,
        scratch_shapes=[pltpu.VMEM(BUF, BF)] * 12
        + [
            pltpu.VMEM(b, BF)
            for wide in (X_WIDE, C_WIDE, X_WIDE, C_WIDE, Y_WIDE)
            for b in token_buffers(wide)
        ]
        + [pltpu.VMEM((4, 128, n), BF) for n in X_WIDE + C_WIDE + Y_WIDE]
        + [pltpu.VMEM(gu_shape, BF), pltpu.VMEM(BUF, BF)] * 2
        + [pltpu.VMEM((ROWS, 1024), BF)] * 2
        + [pltpu.VMEM((ROWS, 512), BF), pltpu.VMEM((ROWS, 1024), BF)]
        + [pltpu.VMEM((3, N + 1, 16, 256), F32)]
        + [pltpu.VMEM((3, 4, 8, N), jnp.int32), pltpu.VMEM((3, 4, 8, N), F32)]
        + [pltpu.VMEM((3, N, N), BF), pltpu.VMEM((3, 3, N, N), BF)]
        + [pltpu.VMEM((512, 384), F32), pltpu.VMEM((N, 1024), F32)]
        + semaphores(7)
        + bounce_buffers(),
        compiler_params=pltpu.CompilerParams(
            collective_id=0, has_side_effects=True, vmem_limit_bytes=63 * mega
        ),
    )(table, swap, pick, routes.T, gate_weights.T, tokens, cotangent, *arrays)
    layer_out, home_gu, home_dn, m_gu, m_dn, q_gu, q_dn = outs[:7]

    def pieces(rows):
        return pl.BlockSpec((1, 2, 2, rows, 1024), lambda i: (i // 2, i % 2, 0, 0, 0))

    def whole(rows):
        return pl.BlockSpec((1, rows, 1024), lambda i: (0, i, 0))

    new = pl.pallas_call(
        weights_kernel,
        grid=(8,),
        out_shape=[shape(1, 1024, 1024)] * 3 + [shape(1, 512, 1024)] * 3,
        in_specs=[pieces(32)] * 3 + [pieces(16)] * 3,
        out_specs=[whole(128)] * 3 + [whole(64)] * 3,
        compiler_params=pltpu.CompilerParams(vmem_limit_bytes=60 * mega),
    )(home_gu, m_gu, q_gu, home_dn, m_dn, q_dn)
    return layer_out, new[0], new[3], new[1], new[4], new[2], new[5]


def solution(mesh):
    tok = P("ep", None)
    slot = P("ep", None, None)
    return jax.shard_map(
        shards,
        mesh=mesh,
        in_specs=(tok,) * 4 + (P(), P()) + (slot,) * 6,
        out_specs=(tok,) + (slot,) * 6,
        check_vma=False,
    )
```

```python
import jax
import jax.numpy as jnp
import numpy as np
from jax import lax
from jax.sharding import PartitionSpec as P
from jax.experimental import pallas as pl
from jax.experimental.pallas import tpu as pltpu

N = 128
CAP = 12
ROWS = N * CAP
BF = jnp.bfloat16
F32 = jnp.float32
MESH = pl.DeviceIdType.MESH

ORDER = (("x", "y", "z"), ("y", "z", "x"), ("z", "x", "y"))
BUF = (4, 4, 2, 16, 1024)
SLOTS = (2, 3, 2)

X_WIDE = (384, 384, 256)
C_WIDE = (384, 256, 384)
Y_WIDE = (256, 384, 384)
STEP = {"z": 32, "y": 8, "x": 2}


def coordinates():
    me = lax.axis_index("ep")
    return {"z": me // 32, "y": (me // 8) % 4, "x": (me // 2) % 4, "c": me % 2}


def device(at, **moved):
    q = {**at, **moved}
    return (q["z"] * 32 + q["y"] * 8 + q["x"] * 2 + q["c"],)


def cut(ref, rows, **kw):
    if "x" in kw:
        cols = pl.ds(pl.multiple_of(kw["x"] * 256, 256), 256)
    else:
        cols = slice(None)
    every = slice(None)
    row = every if rows is None else pl.ds(rows, 16)
    return ref.at[kw.get("z", every), kw.get("y", every), kw.get("c", every), row, cols]


def bounce_shape(stream, phase):
    size = {"z": 4, "y": 4, "c": 2, "x": 4}
    size[ORDER[stream][phase]] = None
    if phase == 0:
        size["c"] = None
    lead = tuple(size[a] for a in "zyc" if size[a])
    return lead + (16, 1024 if size["x"] else 256)


def enter(at):
    bar = pltpu.get_barrier_semaphore()
    pl.semaphore_signal(bar, inc=1, device_id=device(at, c=1 - at["c"]), device_id_type=MESH)
    for axis in "zyx":
        for d in (1, 2, 3):
            for dc in (0, 1):
                there = {axis: (at[axis] + d) % 4, "c": (at["c"] + dc) % 2}
                pl.semaphore_signal(
                    bar, inc=1, device_id=device(at, **there), device_id_type=MESH
                )
    pl.semaphore_wait(bar, 19)


class Exchanges:
    def __init__(self, at, stages, near, sends, receives, bounces, bounce_sems):
        self.at, self.stages, self.near = at, stages, near
        self.sends, self.receives = sends, receives
        self.bounces, self.bounce_sems = bounces, bounce_sems
        self.held = {}
        self.drained = set()
        self.ids = {g: i for i, g in enumerate(stages)}

    def start(self, g, phase):
        at, i = self.at, self.ids[g]
        loads = []
        if phase:
            for s in range(3):
                self._arrived(g, s, phase - 1)
        for s in range(3):
            (src, src_rows), (dst, dst_rows) = self.stages[g][s][phase : phase + 2]
            axis = ORDER[s][phase]
            mine = {axis: at[axis]}
            if phase == 0:
                mine["c"] = at["c"]
            if (g, phase) in self.near:
                pltpu.make_async_copy(
                    cut(src, src_rows, **mine),
                    cut(dst, dst_rows, **mine),
                    self.receives.at[i, s, phase],
                ).start()
                continue
            used = {v for k, v in self.held.items() if k[1:] == (s, phase)}
            slot = min(set(range(SLOTS[phase])) - used)
            self.held[g, s, phase] = slot
            n = sum(SLOTS[:phase]) * 3 + slot * 3 + s
            load = pltpu.make_async_copy(
                cut(src, src_rows, **mine), self.bounces[n], self.bounce_sems.at[n]
            )
            load.start()
            loads.append((load, n, cut(dst, dst_rows, **mine), s))
        for d in (2, 1, 3, 0):
            for dc in (0, 1) if phase == 0 else (0,):
                if d == 0 and dc == 0:
                    continue
                for s in range(3):
                    (src, src_rows), (dst, dst_rows) = self.stages[g][s][phase : phase + 2]
                    axis = ORDER[s][phase]
                    mine = {axis: at[axis]}
                    there = {axis: (at[axis] + d) % 4}
                    if phase == 0:
                        mine["c"] = at["c"]
                        there["c"] = (at["c"] + dc) % 2
                    pltpu.make_async_remote_copy(
                        cut(src, src_rows, **there),
                        cut(dst, dst_rows, **mine),
                        self.sends.at[i, s, phase],
                        self.receives.at[i, s, phase],
                        device_id=device(at, **there),
                        device_id_type=MESH,
                    ).start()
        for load, n, dst, s in loads:
            load.wait()
            pltpu.make_async_copy(
                self.bounces[n], dst, self.receives.at[i, s, phase]
            ).start()

    def _arrived(self, g, s, phase):
        dst, rows = self.stages[g][s][phase + 1]
        whole = cut(dst, rows)
        pltpu.make_async_copy(whole, whole, self.receives.at[self.ids[g], s, phase]).wait()
        self.held.pop((g, s, phase), None)

    def finish(self, g):
        for s in range(3):
            self._arrived(g, s, 2)

    def sent(self, g, phase):
        if (g, phase) in self.drained:
            return
        self.drained.add((g, phase))
        for s in range(3):
            ref, rows = self.stages[g][s][phase + 1]
            row = slice(None) if rows is None else pl.ds(rows, 16)
            part = ref.at[:, :, :, row, pl.ds(0, 768 if phase else 896)]
            pltpu.make_async_copy(part, part, self.sends.at[self.ids[g], s, phase]).wait()

    def drain(self):
        for g in self.ids:
            for phase in range(3):
                self.sent(g, phase)


def spans(wide):
    return [(sum(wide[:s]), wide[s]) for s in range(3)]


class TokenExchanges:
    def __init__(self, at, sends, receives):
        self.at, self.sends, self.receives = at, sends, receives

    def _remote(self, src, dst, there, key, extra=0):
        pltpu.make_async_remote_copy(
            src,
            dst,
            self.sends.at[(*key, extra)],
            self.receives.at[key],
            device_id=device(self.at, **there),
            device_id_type=MESH,
        ).start()

    def ring(self, g, phase, s, pairs, key=None):
        axis = ORDER[s][0]
        for d in (2, 1, 3):
            there = (self.at[axis] + d) % 4
            src, dst = pairs(there)
            self._remote(src, dst, {axis: there}, key or (g, s, phase))

    def second(self, g, phase, src, dst):
        at = self.at
        for d in (2, 1, 3, 0):
            for dc in (0, 1):
                for s in range(3):
                    axis = ORDER[s][1]
                    there = {axis: (at[axis] + d) % 4, "c": (at["c"] + dc) % 2}
                    here = dst[s].at[at[axis], at["c"]]
                    if d == 0 and dc == 0:
                        pltpu.make_async_copy(
                            src[s].at[at[axis], at["c"]], here, self.receives.at[g, s, phase]
                        ).start()
                    else:
                        part = src[s].at[there[axis], there["c"]]
                        self._remote(part, here, there, (g, s, phase), dc)

    def third(self, g, phase, src, dst):
        at = self.at
        for d in (2, 1, 3, 0):
            for s in range(3):
                axis = ORDER[s][2]
                to = (at[axis] + d) % 4
                here = dst[s].at[:, :, at[axis]]
                if d == 0:
                    pltpu.make_async_copy(
                        src[s].at[:, :, to], here, self.receives.at[g, s, phase]
                    ).start()
                else:
                    self._remote(src[s].at[:, :, to], here, {axis: to}, (g, s, phase))

    def arrived(self, g, phase, s, ref):
        pltpu.make_async_copy(ref, ref, self.receives.at[g, s, phase]).wait()

    def left(self, g, phase, s, ref, extra=0):
        pltpu.make_async_copy(ref, ref, self.sends.at[g, s, phase, extra]).wait()


def arrange(swap, land, wide, out):
    def body(g, carry):
        c = g % 2
        for s, (start, n) in enumerate(spans(wide)):
            cols = slice(start, start + n)
            if s == 0:
                out[pl.ds(pl.multiple_of(g * 192, 16), 192), cols] = land[s][g // 2, c].reshape(192, n)
            elif s == 1:
                rows = land[s][g // 2, c].reshape(192, n)
                rows = jnp.dot(swap, rows, preferred_element_type=F32).astype(BF)
                for y in range(4):
                    r = pl.multiple_of(((y * 2 + c) * 4 + g // 2) * 48, 16)
                    out[pl.ds(r, 48), cols] = rows[y * 48 : y * 48 + 48]
            else:
                rows = jnp.concatenate([land[s][x, c, g // 2] for x in range(4)], axis=0)
                rows = jnp.dot(swap, rows, preferred_element_type=F32).astype(BF)
                out[pl.ds(pl.multiple_of(g * 192, 16), 192), cols] = rows
        return carry

    lax.fori_loop(0, 8, body, 0)


def piece_of(ref, table, j):
    full = ref[table[0, j], table[1, j], table[2, j]].astype(F32)
    return sum(full[:, x * 256 : x * 256 + 256] * table[3 + x, j].astype(F32) for x in range(4))


def routing(at, s, routes, gates, ranks, weights):
    lane = lax.broadcasted_iota(jnp.int32, (N, N), 1)
    line = lax.broadcasted_iota(jnp.int32, (N, N), 0)
    first, second, third = ORDER[s]
    slot = (line >> 5) * STEP[second] + ((line >> 4) & 1) + (line & 3) * STEP[third]
    slot = slot + at[first] * STEP[first]
    block = (line >> 2) & 3
    hit = jnp.zeros((N, N), F32)
    gate = jnp.zeros((N, N), F32)
    for b in range(4):
        wanted = jnp.where(block == b, slot, -1)
        for k in range(8):
            named = routes[b, k : k + 1, :] == wanted
            hit = jnp.where(named, 1.0, hit)
            gate = jnp.where(named, gates[b, k : k + 1, :], gate)
    above = jnp.where(line < lane, 1.0, 0.0).astype(BF)
    row = jnp.dot(hit.astype(BF), above, preferred_element_type=F32)
    ranks[...] = jnp.where(hit > 0.0, row + 1.0, 0.0).astype(BF)
    for part in range(3):
        high = gate.astype(BF)
        weights[part] = high
        gate = gate - high.astype(F32)


def placed(pick, ranks, g):
    lines = pl.ds(pl.multiple_of(g * 16, 16), 16)
    got = jnp.dot(pick, ranks[lines], preferred_element_type=F32)
    i = lax.broadcasted_iota(jnp.int32, (192, N), 0).astype(F32)
    rank = i - jnp.floor((i + 0.5) * (1.0 / CAP)) * CAP + 1.0
    return [got[k * 192 : k * 192 + 192] == rank for k in range(4)]


def weighed(pick, weights, here, g):
    lines = pl.ds(pl.multiple_of(g * 16, 16), 16)
    got = sum(
        jnp.dot(pick, weights[part, lines], preferred_element_type=F32) for part in range(3)
    )
    return jnp.concatenate(
        [jnp.where(here[k], got[k * 192 : k * 192 + 192], 0.0) for k in range(4)], axis=1
    )


def step_kernel(*refs):
    table, swap, pick, routes, gates, tokens, cotangent = refs[:7]
    w_gu, w_dn, m_gu, m_dn, q_gu, q_dn = refs[7:13]
    layer_out, home_gu, home_dn = refs[13:16]
    new_m, new_q = refs[16:18], refs[18:20]
    m_far, q_far = refs[20:23], refs[23:26]
    mids = refs[26:68]
    x_mid, c_mid, y_mid = refs[68:71], refs[71:74], refs[74:77]
    scratch = refs[77:]
    w_land, g_land, w_stage, old = (scratch[i : i + 3] for i in range(0, 12, 3))
    x_send, c_send, x_land, c_land, y_land = (scratch[i : i + 3] for i in range(12, 27, 3))
    x_all, c_all, y_parts = (scratch[i : i + 3] for i in range(27, 36, 3))
    gu, dn, g_gu, g_dn, xs, cs, hidden, d_pre, sums = scratch[36:45]
    all_routes, all_gates, ranks, weights, total, own = scratch[45:51]
    sends, receives, bounce_sems, copy_sem, t_sends, t_receives = scratch[51:57]
    bounces = scratch[57:]
    m_send, q_send = w_stage, w_land
    y_send = (x_send[2], x_send[0], x_send[1])
    my_parts = (x_all[2], x_all[0], x_all[1])
    y_kept = x_land[0]

    def raw(a, b):
        return [(a, 0), (a, 16), (b, None)]

    def plain(group):
        return [(r, None) for r in group]

    ends = {
        "w": (raw(w_gu, w_dn), plain(w_land)),
        "home": (plain(w_stage), raw(gu, dn)),
        "m": (raw(m_gu, m_dn), plain(m_far)),
        "q": (raw(q_gu, q_dn), plain(q_far)),
        "g": (raw(g_gu, g_dn), plain(g_land)),
        "new_m": (plain(m_send), raw(*new_m)),
        "new_q": (plain(q_send), raw(*new_q)),
    }
    stages = {}
    for i, (g, (first, end)) in enumerate(ends.items()):
        stages[g] = [
            (first[s], (mids[i * 6 + s], None), (mids[i * 6 + 3 + s], None), end[s])
            for s in range(3)
        ]
    at = coordinates()
    enter(at)
    near = {("w", 2), ("home", 0), ("home", 2), ("g", 0), ("g", 2), ("new_m", 0), ("new_q", 0)}
    ex = Exchanges(at, stages, near, sends, receives, bounces, bounce_sems)
    tx = TokenExchanges(at, t_sends, t_receives)

    def gather(g, rows, everyone, wide):
        for s, (start, n) in enumerate(spans(wide)):
            here = everyone[s].at[at[ORDER[s][0]]]
            mine = rows.at[:, pl.ds(start, n)]
            tx.ring(g, 0, s, lambda there, mine=mine, here=here: (mine, here))

    def keep_own(rows, everyone, wide):
        for s, (start, n) in enumerate(spans(wide)):
            everyone[s][at[ORDER[s][0]]] = rows[:, start : start + n]

    def gather_tables():
        for s in range(3):
            me = at[ORDER[s][0]]
            for k, (mine, everyone) in enumerate(((routes, all_routes), (gates, all_gates))):
                here = everyone.at[s, me]
                tx.ring(0, 0, s, lambda there, mine=mine, here=here: (mine, here), (3, s, k))
                everyone[s, me] = mine[...]

    def dispatch(s):
        def body(g, carry):
            here = placed(pick[...], ranks.at[s], g)
            place = jnp.concatenate(
                [jnp.where(h, 1.0, 0.0).astype(BF) for h in here], axis=1
            )
            gate = jnp.sum(weighed(pick[...], weights.at[s], here, g), axis=1, keepdims=True)
            for everyone, out, wide, factor in (
                (x_all, x_send, X_WIDE, None),
                (c_all, c_send, C_WIDE, gate),
            ):
                rows = everyone[s][...].reshape(512, wide[s])
                got = jnp.dot(place, rows, preferred_element_type=F32)
                if factor is not None:
                    got = got * factor
                out[s][g // 2, g % 2] = got.astype(BF).reshape(4, 48, wide[s])
            return carry

        lax.fori_loop(0, 8, body, 0)

    def combine(s):
        n = Y_WIDE[s]
        total[...] = jnp.zeros_like(total)
        over_rows = (((0,), (0,)), ((), ()))

        def body(g, carry):
            here = placed(pick[...], ranks.at[s], g)
            weight = weighed(pick[...], weights.at[s], here, g)
            high = weight.astype(BF)
            low = (weight - high.astype(F32)).astype(BF)
            rows = y_land[s][g // 2, g % 2].reshape(192, n)
            got = lax.dot_general(high, rows, over_rows, preferred_element_type=F32)
            got += lax.dot_general(low, rows, over_rows, preferred_element_type=F32)
            total[:, 0:n] += got
            return carry

        lax.fori_loop(0, 8, body, 0)
        start = spans(Y_WIDE)[s][0]
        for k in range(4):
            my_parts[s][k] = total[k * 128 : k * 128 + 128, 0:n].astype(BF)
        me = at[ORDER[s][0]]
        own[:, start : start + n] = total[pl.ds(pl.multiple_of(me * 128, 128), 128), 0:n]
        tx.ring(2, 2, s, lambda there: (my_parts[s].at[there], y_parts[s].at[me]))

    def each_slot(do):
        def body(i, carry):
            z, y, c = i // 8, (i // 2) % 4, i % 2
            for x in range(4):
                for s in range(3):
                    do(s, (z, y, c, slice(None), slice(x * 256, x * 256 + 256)), i * 4 + x)
            return carry

        lax.fori_loop(0, 32, body, 0)

    def forward(b, carry):
        r = pl.ds(pl.multiple_of(b * 192, 16), 192)
        pre = jnp.zeros((192, 1024), F32)
        for k in range(4):
            pre += jnp.dot(
                xs[r, k * 256 : k * 256 + 256],
                gu[k].reshape(256, 1024),
                preferred_element_type=F32,
            )
        gate, up = pre[:, :512], pre[:, 512:]
        d_hid = jnp.concatenate(
            [
                lax.dot_general(
                    cs[r],
                    dn[k].reshape(128, 1024),
                    (((1,), (1,)), ((), ())),
                    preferred_element_type=F32,
                )
                for k in range(4)
            ],
            axis=1,
        )
        sig = jax.nn.sigmoid(gate)
        act = gate * sig
        h = (act * up).astype(BF)
        hidden[r] = h
        d_pre[r, 0:512] = (d_hid * up * sig * (1.0 + gate * (1.0 - sig))).astype(BF)
        d_pre[r, 512:1024] = (d_hid * act).astype(BF)
        y = jnp.zeros((192, 1024), F32)
        for k in range(4):
            y += jnp.dot(
                h[:, k * 128 : k * 128 + 128],
                dn[k].reshape(128, 1024),
                preferred_element_type=F32,
            )
        y = y.astype(BF)
        (a0, an), (b0, bn), (c0, cn) = spans(Y_WIDE)
        y_send[0][b // 2, b % 2] = y[:, a0 : a0 + an].reshape(4, 48, an)
        y_kept[b // 2, b % 2] = y[:, b0 : b0 + bn].reshape(4, 48, bn)
        rows = jnp.dot(swap[...], y[:, c0 : c0 + cn], preferred_element_type=F32).astype(BF)
        for x in range(4):
            y_send[2][x, b % 2, b // 2] = rows[x * 48 : x * 48 + 48]
        return carry

    def turn(g, carry):
        rows = jnp.concatenate([y_kept[y, g % 2, g // 2] for y in range(4)], axis=0)
        rows = jnp.dot(swap[...], rows, preferred_element_type=F32).astype(BF)
        y_send[1][g // 2, g % 2] = rows.reshape(4, 48, Y_WIDE[1])
        return carry

    def tokens_arrived(g, phase, refs):
        for s in range(3):
            tx.arrived(g, phase, s, refs[s])

    def three(refs):
        return [r.at[pl.ds(0, 3)] for r in refs]

    ex.start("w", 0)
    gather_tables()
    gather(0, tokens, x_all, X_WIDE)
    gather(1, cotangent, c_all, C_WIDE)
    ex.start("m", 0)
    keep_own(tokens, x_all, X_WIDE)
    keep_own(cotangent, c_all, C_WIDE)
    for s in range(3):
        tx.arrived(3, 0, s, all_routes.at[s, pl.ds(0, 3)])
        tx.arrived(3, 1, s, all_gates.at[s, pl.ds(0, 3)])
        routing(at, s, all_routes.at[s], all_gates.at[s], ranks.at[s], weights.at[s])
    tokens_arrived(0, 0, three(x_all))
    tokens_arrived(1, 0, three(c_all))
    dispatch(0)
    ex.start("w", 1)
    dispatch(1)
    dispatch(2)
    tx.second(0, 1, x_send, x_mid)
    ex.start("w", 2)
    tx.second(1, 1, c_send, c_mid)
    ex.finish("w")

    def select(s, here, j):
        w_stage[s][here] = piece_of(w_land[s], table, j).astype(BF)

    each_slot(select)
    ex.start("home", 0)
    tokens_arrived(0, 1, x_mid)
    tx.third(0, 2, x_mid, x_land)
    ex.start("home", 1)
    tokens_arrived(1, 1, c_mid)
    tx.third(1, 2, c_mid, c_land)
    ex.start("home", 2)
    ex.start("m", 1)
    ex.start("q", 0)
    tokens_arrived(0, 2, x_land)
    arrange(swap[...], x_land, X_WIDE, xs)
    tokens_arrived(1, 2, c_land)
    arrange(swap[...], c_land, C_WIDE, cs)
    ex.finish("home")
    keep_gu = pltpu.make_async_copy(gu, home_gu, copy_sem.at[0])
    keep_dn = pltpu.make_async_copy(dn, home_dn, copy_sem.at[1])
    keep_gu.start()
    keep_dn.start()
    for s in range(3):
        tx.left(0, 1, s, x_mid[s].at[pl.ds(0, 3), 0], 0)
        tx.left(0, 1, s, x_mid[s].at[:, 0], 1)
    lax.fori_loop(0, 8, forward, 0)
    ex.start("m", 2)
    ex.start("q", 1)
    lax.fori_loop(0, 8, turn, 0)
    for k in range(4):
        got = lax.dot_general(
            xs[:, k * 256 : k * 256 + 256],
            d_pre[...],
            (((0,), (0,)), ((), ())),
            preferred_element_type=F32,
        )
        g_gu[k] = got.astype(BF).reshape(4, 2, 32, 1024)
        got = lax.dot_general(
            hidden[:, k * 128 : k * 128 + 128],
            cs[...],
            (((0,), (0,)), ((), ())),
            preferred_element_type=F32,
        )
        g_dn[k] = got.astype(BF).reshape(4, 2, 16, 1024)
    ex.start("g", 0)
    tx.third(2, 0, y_send, y_mid)

    def fetch(far, first):
        copies = [
            pltpu.make_async_copy(a, b, copy_sem.at[first + i])
            for i, (a, b) in enumerate(zip(far, old))
        ]
        for f in copies:
            f.start()
        return copies

    ex.start("g", 1)
    ex.start("q", 2)
    ex.finish("m")
    coming = fetch(m_far, 2)
    ex.start("g", 2)
    tokens_arrived(2, 0, y_mid)
    tx.second(2, 1, y_mid, y_land)
    for s in range(3):
        sums[s, N] = jnp.zeros((16, 256), F32)
        tx.left(0, 0, s, x_all[s].at[pl.ds(0, 3)])
    ex.finish("g")

    def add(s, here, j):
        sums[s, j] = g_land[s][here].astype(F32) + sums[s, table[7, j]]

    each_slot(add)
    for f in coming:
        f.wait()
    ex.sent("home", 0)

    def update_first(s, here, j):
        was = piece_of(old[s], table, j)
        m_send[s][here] = (0.9 * was + 0.1 * sums[s, table[8, j]]).astype(BF)

    def update_second(s, here, j):
        was = piece_of(old[s], table, j)
        total = sums[s, table[8, j]]
        q_send[s][here] = (0.95 * was + 0.05 * total * total).astype(BF)

    each_slot(update_first)
    ex.start("new_m", 0)
    ex.finish("q")
    for f in fetch(q_far, 5):
        f.wait()
    each_slot(update_second)
    ex.start("new_q", 0)
    tokens_arrived(2, 1, y_land)
    combine(0)
    ex.start("new_m", 1)
    combine(1)
    ex.start("new_q", 1)
    combine(2)
    ex.start("new_m", 2)
    for s, (start, n) in enumerate(spans(Y_WIDE)):
        tx.arrived(2, 2, s, y_parts[s].at[pl.ds(0, 3)])
        me = at[ORDER[s][0]]
        result = own[:, start : start + n]
        for d in (1, 2, 3):
            result += y_parts[s][(me + d) % 4].astype(F32)
        layer_out[:, start : start + n] = result.astype(BF)
    ex.start("new_q", 2)
    for s in range(3):
        tx.left(1, 0, s, c_all[s].at[pl.ds(0, 3)])
        tx.left(3, 0, s, all_routes.at[s, pl.ds(0, 3)])
        tx.left(3, 1, s, all_gates.at[s, pl.ds(0, 3)])
        tx.left(0, 2, s, x_mid[s].at[:, :, pl.ds(0, 3)])
        tx.left(1, 1, s, c_mid[s].at[pl.ds(0, 3), 0], 0)
        tx.left(1, 1, s, c_mid[s].at[:, 0], 1)
        tx.left(1, 2, s, c_mid[s].at[:, :, pl.ds(0, 3)])
        tx.left(2, 0, s, y_mid[s].at[:, :, pl.ds(0, 3)])
        tx.left(2, 1, s, y_mid[s].at[pl.ds(0, 3), 0], 0)
        tx.left(2, 1, s, y_mid[s].at[:, 0], 1)
        tx.left(2, 2, s, y_parts[s].at[pl.ds(0, 3)])
    ex.finish("new_m")
    ex.finish("new_q")
    ex.drain()
    keep_gu.wait()
    keep_dn.wait()


def weights_kernel(*refs):
    for i in range(2):
        w, m, q = (refs[3 * i + k] for k in range(3))
        new_w, new_m, new_q = (refs[6 + 3 * i + k] for k in range(3))
        rows = new_w.shape[1]
        first, second = m[...].reshape(rows, 1024), q[...].reshape(rows, 1024)
        weight = w[...].reshape(rows, 1024).astype(F32)
        change = 0.01 * first.astype(F32) / (jnp.sqrt(second.astype(F32)) + 1e-8)
        new_w[0] = (weight - change).astype(BF)
        new_m[0] = first
        new_q[0] = second


def shape(*dims, dtype=BF):
    return jax.ShapeDtypeStruct(dims, dtype)


def semaphores(groups):
    dma = pltpu.SemaphoreType.DMA
    return [
        dma((groups, 3, 3)),
        dma((groups, 3, 3)),
        dma((sum(SLOTS) * 3,)),
        dma((8,)),
        dma((4, 3, 3, 2)),
        dma((4, 3, 3)),
    ]


def bounce_buffers():
    return [
        pltpu.VMEM(bounce_shape(s, phase), BF)
        for phase in range(3)
        for _ in range(SLOTS[phase])
        for s in range(3)
    ]


def token_buffers(wide):
    return [(4, 2, 4, 48, n) for n in wide]


def constants():
    i = np.arange(192)
    swap = (i // 12 % 4 * 48 + i // 48 * 12 + i % 12)[:, None] == i[None, :]
    block = np.arange(4)[:, None, None]
    line = np.arange(16)[None, None, :]
    rows = i[None, :, None]
    pick = (rows // 12 % 4 == block) & (line // 4 == block) & (line % 4 == rows // 48)
    return (
        jnp.asarray(swap.astype(np.float32), BF),
        jnp.asarray(pick.reshape(768, 16).astype(np.float32), BF),
    )


def tables(old_experts, source):
    j = jnp.arange(N, dtype=jnp.int32)
    src = source.reshape(4, 4, 4, 2).transpose(0, 1, 3, 2).reshape(N)
    expert = jnp.sum(jnp.where(src[:, None] == j[None, :], old_experts[None, :], 0), axis=1)
    same = expert[:, None] == expert[None, :]
    before = jnp.max(jnp.where(same & (j[None, :] < j[:, None]), j[None, :], -1), axis=1)
    before = jnp.where(before < 0, N, before)
    last = jnp.max(jnp.where(same, j[None, :], -1), axis=1)
    x = (src // 2) % 4
    rows = [src // 32, (src // 8) % 4, src % 2] + [(x == k).astype(jnp.int32) for k in range(4)]
    return jnp.stack(rows + [before, last])


def shards(
    tokens,
    cotangent,
    routes,
    gate_weights,
    old_experts,
    source,
    gate_up_weight,
    down_weight,
    first_gate_up,
    first_down,
    second_gate_up,
    second_down,
):
    table = tables(old_experts, source)
    swap, pick = constants()
    gu_shape, dn_shape = (4, 4, 2, 32, 1024), BUF
    arrays = (
        gate_up_weight.reshape(gu_shape),
        down_weight.reshape(dn_shape),
        first_gate_up.reshape(gu_shape),
        first_down.reshape(dn_shape),
        second_gate_up.reshape(gu_shape),
        second_down.reshape(dn_shape),
    )
    smem = pl.BlockSpec(memory_space=pltpu.SMEM)
    vmem = pl.BlockSpec(memory_space=pltpu.VMEM)
    hbm = pl.BlockSpec(memory_space=pl.ANY)
    gu, buf = shape(*gu_shape), shape(*BUF)
    mega = 1 << 20
    outs = pl.pallas_call(
        step_kernel,
        out_shape=[shape(N, 1024)]
        + [gu, buf] * 3
        + [buf] * 48
        + [shape(*b) for wide in (X_WIDE, C_WIDE, Y_WIDE) for b in token_buffers(wide)],
        in_specs=[smem] + [vmem] * 6 + [hbm] * 6,
        out_specs=[vmem] + [hbm] * 63,
        scratch_shapes=[pltpu.VMEM(BUF, BF)] * 12
        + [
            pltpu.VMEM(b, BF)
            for wide in (X_WIDE, C_WIDE, X_WIDE, C_WIDE, Y_WIDE)
            for b in token_buffers(wide)
        ]
        + [pltpu.VMEM((4, 128, n), BF) for n in X_WIDE + C_WIDE + Y_WIDE]
        + [pltpu.VMEM(gu_shape, BF), pltpu.VMEM(BUF, BF)] * 2
        + [pltpu.VMEM((ROWS, 1024), BF)] * 2
        + [pltpu.VMEM((ROWS, 512), BF), pltpu.VMEM((ROWS, 1024), BF)]
        + [pltpu.VMEM((3, N + 1, 16, 256), F32)]
        + [pltpu.VMEM((3, 4, 8, N), jnp.int32), pltpu.VMEM((3, 4, 8, N), F32)]
        + [pltpu.VMEM((3, N, N), BF), pltpu.VMEM((3, 3, N, N), BF)]
        + [pltpu.VMEM((512, 384), F32), pltpu.VMEM((N, 1024), F32)]
        + semaphores(7)
        + bounce_buffers(),
        compiler_params=pltpu.CompilerParams(
            collective_id=0, has_side_effects=True, vmem_limit_bytes=63 * mega
        ),
    )(table, swap, pick, routes.T, gate_weights.T, tokens, cotangent, *arrays)
    layer_out, home_gu, home_dn, m_gu, m_dn, q_gu, q_dn = outs[:7]

    def pieces(rows):
        return pl.BlockSpec((1, 2, 2, rows, 1024), lambda i: (i // 2, i % 2, 0, 0, 0))

    def whole(rows):
        return pl.BlockSpec((1, rows, 1024), lambda i: (0, i, 0))

    new = pl.pallas_call(
        weights_kernel,
        grid=(8,),
        out_shape=[shape(1, 1024, 1024)] * 3 + [shape(1, 512, 1024)] * 3,
        in_specs=[pieces(32)] * 3 + [pieces(16)] * 3,
        out_specs=[whole(128)] * 3 + [whole(64)] * 3,
        compiler_params=pltpu.CompilerParams(vmem_limit_bytes=60 * mega),
    )(home_gu, m_gu, q_gu, home_dn, m_dn, q_dn)
    return layer_out, new[0], new[3], new[1], new[4], new[2], new[5]


def solution(mesh):
    tok = P("ep", None)
    slot = P("ep", None, None)
    return jax.shard_map(
        shards,
        mesh=mesh,
        in_specs=(tok,) * 4 + (P(), P()) + (slot,) * 6,
        out_specs=(tok,) + (slot,) * 6,
        check_vma=False,
    )
```

```python
import jax
import jax.numpy as jnp
import numpy as np
from jax import lax
from jax.sharding import PartitionSpec as P
from jax.experimental import pallas as pl
from jax.experimental.pallas import tpu as pltpu

N = 128
CAP = 12
ROWS = N * CAP
BF = jnp.bfloat16
F32 = jnp.float32
MESH = pl.DeviceIdType.MESH

ORDER = (("x", "y", "z"), ("y", "z", "x"), ("z", "x", "y"))
BUF = (4, 4, 2, 16, 1024)
SLOTS = (2, 3, 2)

X_WIDE = (384, 384, 256)
C_WIDE = (384, 256, 384)
Y_WIDE = (256, 384, 384)
STEP = {"z": 32, "y": 8, "x": 2}


def coordinates():
    me = lax.axis_index("ep")
    return {"z": me // 32, "y": (me // 8) % 4, "x": (me // 2) % 4, "c": me % 2}


def device(at, **moved):
    q = {**at, **moved}
    return (q["z"] * 32 + q["y"] * 8 + q["x"] * 2 + q["c"],)


def cut(ref, rows, **kw):
    if "x" in kw:
        cols = pl.ds(pl.multiple_of(kw["x"] * 256, 256), 256)
    else:
        cols = slice(None)
    every = slice(None)
    row = every if rows is None else pl.ds(rows, 16)
    return ref.at[kw.get("z", every), kw.get("y", every), kw.get("c", every), row, cols]


def bounce_shape(stream, phase):
    size = {"z": 4, "y": 4, "c": 2, "x": 4}
    size[ORDER[stream][phase]] = None
    if phase == 0:
        size["c"] = None
    lead = tuple(size[a] for a in "zyc" if size[a])
    return lead + (16, 1024 if size["x"] else 256)


def enter(at):
    bar = pltpu.get_barrier_semaphore()
    pl.semaphore_signal(bar, inc=1, device_id=device(at, c=1 - at["c"]), device_id_type=MESH)
    for axis in "zyx":
        for d in (1, 2, 3):
            for dc in (0, 1):
                there = {axis: (at[axis] + d) % 4, "c": (at["c"] + dc) % 2}
                pl.semaphore_signal(
                    bar, inc=1, device_id=device(at, **there), device_id_type=MESH
                )
    pl.semaphore_wait(bar, 19)


class Exchanges:
    def __init__(self, at, stages, near, sends, receives, bounces, bounce_sems):
        self.at, self.stages, self.near = at, stages, near
        self.sends, self.receives = sends, receives
        self.bounces, self.bounce_sems = bounces, bounce_sems
        self.held = {}
        self.drained = set()
        self.ids = {g: i for i, g in enumerate(stages)}

    def start(self, g, phase):
        at, i = self.at, self.ids[g]
        loads = []
        if phase:
            for s in range(3):
                self._arrived(g, s, phase - 1)
        for s in range(3):
            (src, src_rows), (dst, dst_rows) = self.stages[g][s][phase : phase + 2]
            axis = ORDER[s][phase]
            mine = {axis: at[axis]}
            if phase == 0:
                mine["c"] = at["c"]
            if (g, phase) in self.near:
                pltpu.make_async_copy(
                    cut(src, src_rows, **mine),
                    cut(dst, dst_rows, **mine),
                    self.receives.at[i, s, phase],
                ).start()
                continue
            used = {v for k, v in self.held.items() if k[1:] == (s, phase)}
            slot = min(set(range(SLOTS[phase])) - used)
            self.held[g, s, phase] = slot
            n = sum(SLOTS[:phase]) * 3 + slot * 3 + s
            load = pltpu.make_async_copy(
                cut(src, src_rows, **mine), self.bounces[n], self.bounce_sems.at[n]
            )
            load.start()
            loads.append((load, n, cut(dst, dst_rows, **mine), s))
        for d in (2, 1, 3, 0):
            for dc in (0, 1) if phase == 0 else (0,):
                if d == 0 and dc == 0:
                    continue
                for s in range(3):
                    (src, src_rows), (dst, dst_rows) = self.stages[g][s][phase : phase + 2]
                    axis = ORDER[s][phase]
                    mine = {axis: at[axis]}
                    there = {axis: (at[axis] + d) % 4}
                    if phase == 0:
                        mine["c"] = at["c"]
                        there["c"] = (at["c"] + dc) % 2
                    pltpu.make_async_remote_copy(
                        cut(src, src_rows, **there),
                        cut(dst, dst_rows, **mine),
                        self.sends.at[i, s, phase],
                        self.receives.at[i, s, phase],
                        device_id=device(at, **there),
                        device_id_type=MESH,
                    ).start()
        for load, n, dst, s in loads:
            load.wait()
            pltpu.make_async_copy(
                self.bounces[n], dst, self.receives.at[i, s, phase]
            ).start()

    def _arrived(self, g, s, phase):
        dst, rows = self.stages[g][s][phase + 1]
        whole = cut(dst, rows)
        pltpu.make_async_copy(whole, whole, self.receives.at[self.ids[g], s, phase]).wait()
        self.held.pop((g, s, phase), None)

    def finish(self, g):
        for s in range(3):
            self._arrived(g, s, 2)

    def sent(self, g, phase):
        if (g, phase) in self.drained:
            return
        self.drained.add((g, phase))
        for s in range(3):
            ref, rows = self.stages[g][s][phase + 1]
            row = slice(None) if rows is None else pl.ds(rows, 16)
            part = ref.at[:, :, :, row, pl.ds(0, 768 if phase else 896)]
            pltpu.make_async_copy(part, part, self.sends.at[self.ids[g], s, phase]).wait()

    def drain(self):
        for g in self.ids:
            for phase in range(3):
                self.sent(g, phase)


def spans(wide):
    return [(sum(wide[:s]), wide[s]) for s in range(3)]


class TokenExchanges:
    def __init__(self, at, sends, receives):
        self.at, self.sends, self.receives = at, sends, receives

    def _remote(self, src, dst, there, key, extra=0):
        pltpu.make_async_remote_copy(
            src,
            dst,
            self.sends.at[(*key, extra)],
            self.receives.at[key],
            device_id=device(self.at, **there),
            device_id_type=MESH,
        ).start()

    def ring(self, g, phase, s, pairs, key=None):
        axis = ORDER[s][0]
        for d in (2, 1, 3):
            there = (self.at[axis] + d) % 4
            src, dst = pairs(there)
            self._remote(src, dst, {axis: there}, key or (g, s, phase))

    def second(self, g, phase, src, dst):
        at = self.at
        for d in (2, 1, 3, 0):
            for dc in (0, 1):
                for s in range(3):
                    axis = ORDER[s][1]
                    there = {axis: (at[axis] + d) % 4, "c": (at["c"] + dc) % 2}
                    here = dst[s].at[at[axis], at["c"]]
                    if d == 0 and dc == 0:
                        pltpu.make_async_copy(
                            src[s].at[at[axis], at["c"]], here, self.receives.at[g, s, phase]
                        ).start()
                    else:
                        part = src[s].at[there[axis], there["c"]]
                        self._remote(part, here, there, (g, s, phase), dc)

    def third(self, g, phase, src, dst):
        at = self.at
        for d in (2, 1, 3, 0):
            for s in range(3):
                axis = ORDER[s][2]
                to = (at[axis] + d) % 4
                here = dst[s].at[:, :, at[axis]]
                if d == 0:
                    pltpu.make_async_copy(
                        src[s].at[:, :, to], here, self.receives.at[g, s, phase]
                    ).start()
                else:
                    self._remote(src[s].at[:, :, to], here, {axis: to}, (g, s, phase))

    def arrived(self, g, phase, s, ref):
        pltpu.make_async_copy(ref, ref, self.receives.at[g, s, phase]).wait()

    def left(self, g, phase, s, ref, extra=0):
        pltpu.make_async_copy(ref, ref, self.sends.at[g, s, phase, extra]).wait()


def arrange(swap, land, wide, out):
    def body(g, carry):
        c = g % 2
        for s, (start, n) in enumerate(spans(wide)):
            cols = slice(start, start + n)
            if s == 0:
                out[pl.ds(pl.multiple_of(g * 192, 16), 192), cols] = land[s][g // 2, c].reshape(192, n)
            elif s == 1:
                rows = land[s][g // 2, c].reshape(192, n)
                rows = jnp.dot(swap, rows, preferred_element_type=F32).astype(BF)
                for y in range(4):
                    r = pl.multiple_of(((y * 2 + c) * 4 + g // 2) * 48, 16)
                    out[pl.ds(r, 48), cols] = rows[y * 48 : y * 48 + 48]
            else:
                rows = jnp.concatenate([land[s][x, c, g // 2] for x in range(4)], axis=0)
                rows = jnp.dot(swap, rows, preferred_element_type=F32).astype(BF)
                out[pl.ds(pl.multiple_of(g * 192, 16), 192), cols] = rows
        return carry

    lax.fori_loop(0, 8, body, 0)


def piece_of(ref, table, j):
    full = ref[table[0, j], table[1, j], table[2, j]].astype(F32)
    return sum(full[:, x * 256 : x * 256 + 256] * table[3 + x, j].astype(F32) for x in range(4))


def routing(at, s, routes, gates, ranks, weights):
    lane = lax.broadcasted_iota(jnp.int32, (N, N), 1)
    line = lax.broadcasted_iota(jnp.int32, (N, N), 0)
    first, second, third = ORDER[s]
    slot = (line >> 5) * STEP[second] + ((line >> 4) & 1) + (line & 3) * STEP[third]
    slot = slot + at[first] * STEP[first]
    block = (line >> 2) & 3
    hit = jnp.zeros((N, N), F32)
    gate = jnp.zeros((N, N), F32)
    for b in range(4):
        wanted = jnp.where(block == b, slot, -1)
        for k in range(8):
            named = routes[b, k : k + 1, :] == wanted
            hit = jnp.where(named, 1.0, hit)
            gate = jnp.where(named, gates[b, k : k + 1, :], gate)
    above = jnp.where(line < lane, 1.0, 0.0).astype(BF)
    row = jnp.dot(hit.astype(BF), above, preferred_element_type=F32)
    ranks[...] = jnp.where(hit > 0.0, row + 1.0, 0.0).astype(BF)
    for part in range(3):
        high = gate.astype(BF)
        weights[part] = high
        gate = gate - high.astype(F32)


def placed(pick, ranks, g):
    lines = pl.ds(pl.multiple_of(g * 16, 16), 16)
    got = jnp.dot(pick, ranks[lines], preferred_element_type=F32)
    i = lax.broadcasted_iota(jnp.int32, (192, N), 0).astype(F32)
    rank = i - jnp.floor((i + 0.5) * (1.0 / CAP)) * CAP + 1.0
    return [got[k * 192 : k * 192 + 192] == rank for k in range(4)]


def weighed(pick, weights, here, g):
    lines = pl.ds(pl.multiple_of(g * 16, 16), 16)
    got = sum(
        jnp.dot(pick, weights[part, lines], preferred_element_type=F32) for part in range(3)
    )
    return jnp.concatenate(
        [jnp.where(here[k], got[k * 192 : k * 192 + 192], 0.0) for k in range(4)], axis=1
    )


def step_kernel(*refs):
    table, swap, pick, routes, gates, tokens, cotangent = refs[:7]
    w_gu, w_dn, m_gu, m_dn, q_gu, q_dn = refs[7:13]
    layer_out, home_gu, home_dn = refs[13:16]
    new_m, new_q = refs[16:18], refs[18:20]
    m_far, q_far = refs[20:23], refs[23:26]
    mids = refs[26:68]
    x_mid, c_mid, y_mid = refs[68:71], refs[71:74], refs[74:77]
    scratch = refs[77:]
    w_land, g_land, w_stage, old = (scratch[i : i + 3] for i in range(0, 12, 3))
    x_send, c_send, x_land, c_land, y_land = (scratch[i : i + 3] for i in range(12, 27, 3))
    x_all, c_all, y_parts = (scratch[i : i + 3] for i in range(27, 36, 3))
    gu, dn, g_gu, g_dn, xs, cs, hidden, d_pre, sums = scratch[36:45]
    all_routes, all_gates, ranks, weights, total, own = scratch[45:51]
    sends, receives, bounce_sems, copy_sem, t_sends, t_receives = scratch[51:57]
    bounces = scratch[57:]
    m_send, q_send = w_stage, w_land
    y_send = (x_send[2], x_send[0], x_send[1])
    my_parts = (x_all[2], x_all[0], x_all[1])
    y_kept = x_land[0]

    def raw(a, b):
        return [(a, 0), (a, 16), (b, None)]

    def plain(group):
        return [(r, None) for r in group]

    ends = {
        "w": (raw(w_gu, w_dn), plain(w_land)),
        "home": (plain(w_stage), raw(gu, dn)),
        "m": (raw(m_gu, m_dn), plain(m_far)),
        "q": (raw(q_gu, q_dn), plain(q_far)),
        "g": (raw(g_gu, g_dn), plain(g_land)),
        "new_m": (plain(m_send), raw(*new_m)),
        "new_q": (plain(q_send), raw(*new_q)),
    }
    stages = {}
    for i, (g, (first, end)) in enumerate(ends.items()):
        stages[g] = [
            (first[s], (mids[i * 6 + s], None), (mids[i * 6 + 3 + s], None), end[s])
            for s in range(3)
        ]
    at = coordinates()
    enter(at)
    near = {("w", 2), ("home", 0), ("home", 2), ("g", 0), ("g", 2), ("new_m", 0), ("new_q", 0)}
    ex = Exchanges(at, stages, near, sends, receives, bounces, bounce_sems)
    tx = TokenExchanges(at, t_sends, t_receives)

    def gather(g, rows, everyone, wide):
        for s, (start, n) in enumerate(spans(wide)):
            here = everyone[s].at[at[ORDER[s][0]]]
            mine = rows.at[:, pl.ds(start, n)]
            tx.ring(g, 0, s, lambda there, mine=mine, here=here: (mine, here))

    def keep_own(rows, everyone, wide):
        for s, (start, n) in enumerate(spans(wide)):
            everyone[s][at[ORDER[s][0]]] = rows[:, start : start + n]

    def gather_tables():
        for s in range(3):
            me = at[ORDER[s][0]]
            for k, (mine, everyone) in enumerate(((routes, all_routes), (gates, all_gates))):
                here = everyone.at[s, me]
                tx.ring(0, 0, s, lambda there, mine=mine, here=here: (mine, here), (3, s, k))
                everyone[s, me] = mine[...]

    def dispatch(s):
        def body(g, carry):
            here = placed(pick[...], ranks.at[s], g)
            place = jnp.concatenate(
                [jnp.where(h, 1.0, 0.0).astype(BF) for h in here], axis=1
            )
            gate = jnp.sum(weighed(pick[...], weights.at[s], here, g), axis=1, keepdims=True)
            for everyone, out, wide, factor in (
                (x_all, x_send, X_WIDE, None),
                (c_all, c_send, C_WIDE, gate),
            ):
                rows = everyone[s][...].reshape(512, wide[s])
                got = jnp.dot(place, rows, preferred_element_type=F32)
                if factor is not None:
                    got = got * factor
                out[s][g // 2, g % 2] = got.astype(BF).reshape(4, 48, wide[s])
            return carry

        lax.fori_loop(0, 8, body, 0)

    def combine(s):
        n = Y_WIDE[s]
        total[...] = jnp.zeros_like(total)
        over_rows = (((0,), (0,)), ((), ()))

        def body(g, carry):
            here = placed(pick[...], ranks.at[s], g)
            weight = weighed(pick[...], weights.at[s], here, g)
            high = weight.astype(BF)
            low = (weight - high.astype(F32)).astype(BF)
            rows = y_land[s][g // 2, g % 2].reshape(192, n)
            got = lax.dot_general(high, rows, over_rows, preferred_element_type=F32)
            got += lax.dot_general(low, rows, over_rows, preferred_element_type=F32)
            total[:, 0:n] += got
            return carry

        lax.fori_loop(0, 8, body, 0)
        start = spans(Y_WIDE)[s][0]
        for k in range(4):
            my_parts[s][k] = total[k * 128 : k * 128 + 128, 0:n].astype(BF)
        me = at[ORDER[s][0]]
        own[:, start : start + n] = total[pl.ds(pl.multiple_of(me * 128, 128), 128), 0:n]
        tx.ring(2, 2, s, lambda there: (my_parts[s].at[there], y_parts[s].at[me]))

    def each_slot(do):
        def body(i, carry):
            z, y, c = i // 8, (i // 2) % 4, i % 2
            for x in range(4):
                for s in range(3):
                    do(s, (z, y, c, slice(None), slice(x * 256, x * 256 + 256)), i * 4 + x)
            return carry

        lax.fori_loop(0, 32, body, 0)

    def forward(b, carry):
        r = pl.ds(pl.multiple_of(b * 192, 16), 192)
        pre = jnp.zeros((192, 1024), F32)
        for k in range(4):
            pre += jnp.dot(
                xs[r, k * 256 : k * 256 + 256],
                gu[k].reshape(256, 1024),
                preferred_element_type=F32,
            )
        gate, up = pre[:, :512], pre[:, 512:]
        d_hid = jnp.concatenate(
            [
                lax.dot_general(
                    cs[r],
                    dn[k].reshape(128, 1024),
                    (((1,), (1,)), ((), ())),
                    preferred_element_type=F32,
                )
                for k in range(4)
            ],
            axis=1,
        )
        sig = jax.nn.sigmoid(gate)
        act = gate * sig
        h = (act * up).astype(BF)
        hidden[r] = h
        d_pre[r, 0:512] = (d_hid * up * sig * (1.0 + gate * (1.0 - sig))).astype(BF)
        d_pre[r, 512:1024] = (d_hid * act).astype(BF)
        y = jnp.zeros((192, 1024), F32)
        for k in range(4):
            y += jnp.dot(
                h[:, k * 128 : k * 128 + 128],
                dn[k].reshape(128, 1024),
                preferred_element_type=F32,
            )
        y = y.astype(BF)
        (a0, an), (b0, bn), (c0, cn) = spans(Y_WIDE)
        y_send[0][b // 2, b % 2] = y[:, a0 : a0 + an].reshape(4, 48, an)
        y_kept[b // 2, b % 2] = y[:, b0 : b0 + bn].reshape(4, 48, bn)
        rows = jnp.dot(swap[...], y[:, c0 : c0 + cn], preferred_element_type=F32).astype(BF)
        for x in range(4):
            y_send[2][x, b % 2, b // 2] = rows[x * 48 : x * 48 + 48]
        return carry

    def turn(g, carry):
        rows = jnp.concatenate([y_kept[y, g % 2, g // 2] for y in range(4)], axis=0)
        rows = jnp.dot(swap[...], rows, preferred_element_type=F32).astype(BF)
        y_send[1][g // 2, g % 2] = rows.reshape(4, 48, Y_WIDE[1])
        return carry

    def tokens_arrived(g, phase, refs):
        for s in range(3):
            tx.arrived(g, phase, s, refs[s])

    def three(refs):
        return [r.at[pl.ds(0, 3)] for r in refs]

    ex.start("w", 0)
    gather_tables()
    gather(0, tokens, x_all, X_WIDE)
    gather(1, cotangent, c_all, C_WIDE)
    ex.start("m", 0)
    keep_own(tokens, x_all, X_WIDE)
    keep_own(cotangent, c_all, C_WIDE)
    for s in range(3):
        tx.arrived(3, 0, s, all_routes.at[s, pl.ds(0, 3)])
        tx.arrived(3, 1, s, all_gates.at[s, pl.ds(0, 3)])
        routing(at, s, all_routes.at[s], all_gates.at[s], ranks.at[s], weights.at[s])
    tokens_arrived(0, 0, three(x_all))
    tokens_arrived(1, 0, three(c_all))
    dispatch(0)
    ex.start("w", 1)
    dispatch(1)
    dispatch(2)
    tx.second(0, 1, x_send, x_mid)
    ex.start("w", 2)
    tx.second(1, 1, c_send, c_mid)
    ex.finish("w")

    def select(s, here, j):
        w_stage[s][here] = piece_of(w_land[s], table, j).astype(BF)

    each_slot(select)
    ex.start("home", 0)
    tokens_arrived(0, 1, x_mid)
    tx.third(0, 2, x_mid, x_land)
    ex.start("home", 1)
    tokens_arrived(1, 1, c_mid)
    tx.third(1, 2, c_mid, c_land)
    ex.start("home", 2)
    ex.start("m", 1)
    ex.start("q", 0)
    tokens_arrived(0, 2, x_land)
    arrange(swap[...], x_land, X_WIDE, xs)
    tokens_arrived(1, 2, c_land)
    arrange(swap[...], c_land, C_WIDE, cs)
    ex.finish("home")
    keep_gu = pltpu.make_async_copy(gu, home_gu, copy_sem.at[0])
    keep_dn = pltpu.make_async_copy(dn, home_dn, copy_sem.at[1])
    keep_gu.start()
    keep_dn.start()
    for s in range(3):
        tx.left(0, 1, s, x_mid[s].at[pl.ds(0, 3), 0], 0)
        tx.left(0, 1, s, x_mid[s].at[:, 0], 1)
    lax.fori_loop(0, 4, forward, 0)
    ex.start("m", 2)
    lax.fori_loop(4, 8, forward, 0)
    ex.start("q", 1)
    lax.fori_loop(0, 8, turn, 0)
    for k in range(4):
        got = lax.dot_general(
            xs[:, k * 256 : k * 256 + 256],
            d_pre[...],
            (((0,), (0,)), ((), ())),
            preferred_element_type=F32,
        )
        g_gu[k] = got.astype(BF).reshape(4, 2, 32, 1024)
        got = lax.dot_general(
            hidden[:, k * 128 : k * 128 + 128],
            cs[...],
            (((0,), (0,)), ((), ())),
            preferred_element_type=F32,
        )
        g_dn[k] = got.astype(BF).reshape(4, 2, 16, 1024)
    ex.start("g", 0)
    tx.third(2, 0, y_send, y_mid)

    def fetch(far, first):
        copies = [
            pltpu.make_async_copy(a, b, copy_sem.at[first + i])
            for i, (a, b) in enumerate(zip(far, old))
        ]
        for f in copies:
            f.start()
        return copies

    ex.start("g", 1)
    ex.start("q", 2)
    ex.finish("m")
    coming = fetch(m_far, 2)
    ex.start("g", 2)
    tokens_arrived(2, 0, y_mid)
    tx.second(2, 1, y_mid, y_land)
    for s in range(3):
        sums[s, N] = jnp.zeros((16, 256), F32)
        tx.left(0, 0, s, x_all[s].at[pl.ds(0, 3)])
    ex.finish("g")

    def add(s, here, j):
        sums[s, j] = g_land[s][here].astype(F32) + sums[s, table[7, j]]

    each_slot(add)
    for f in coming:
        f.wait()
    ex.sent("home", 0)

    def update_first(s, here, j):
        was = piece_of(old[s], table, j)
        m_send[s][here] = (0.9 * was + 0.1 * sums[s, table[8, j]]).astype(BF)

    def update_second(s, here, j):
        was = piece_of(old[s], table, j)
        total = sums[s, table[8, j]]
        q_send[s][here] = (0.95 * was + 0.05 * total * total).astype(BF)

    each_slot(update_first)
    ex.start("new_m", 0)
    ex.finish("q")
    for f in fetch(q_far, 5):
        f.wait()
    each_slot(update_second)
    ex.start("new_q", 0)
    tokens_arrived(2, 1, y_land)
    combine(0)
    ex.start("new_m", 1)
    combine(1)
    ex.start("new_q", 1)
    combine(2)
    ex.start("new_m", 2)
    for s, (start, n) in enumerate(spans(Y_WIDE)):
        tx.arrived(2, 2, s, y_parts[s].at[pl.ds(0, 3)])
        me = at[ORDER[s][0]]
        result = own[:, start : start + n]
        for d in (1, 2, 3):
            result += y_parts[s][(me + d) % 4].astype(F32)
        layer_out[:, start : start + n] = result.astype(BF)
    ex.start("new_q", 2)
    for s in range(3):
        tx.left(1, 0, s, c_all[s].at[pl.ds(0, 3)])
        tx.left(3, 0, s, all_routes.at[s, pl.ds(0, 3)])
        tx.left(3, 1, s, all_gates.at[s, pl.ds(0, 3)])
        tx.left(0, 2, s, x_mid[s].at[:, :, pl.ds(0, 3)])
        tx.left(1, 1, s, c_mid[s].at[pl.ds(0, 3), 0], 0)
        tx.left(1, 1, s, c_mid[s].at[:, 0], 1)
        tx.left(1, 2, s, c_mid[s].at[:, :, pl.ds(0, 3)])
        tx.left(2, 0, s, y_mid[s].at[:, :, pl.ds(0, 3)])
        tx.left(2, 1, s, y_mid[s].at[pl.ds(0, 3), 0], 0)
        tx.left(2, 1, s, y_mid[s].at[:, 0], 1)
        tx.left(2, 2, s, y_parts[s].at[pl.ds(0, 3)])
    ex.finish("new_m")
    ex.finish("new_q")
    ex.drain()
    keep_gu.wait()
    keep_dn.wait()


def weights_kernel(*refs):
    for i in range(2):
        w, m, q = (refs[3 * i + k] for k in range(3))
        new_w, new_m, new_q = (refs[6 + 3 * i + k] for k in range(3))
        rows = new_w.shape[1]
        first, second = m[...].reshape(rows, 1024), q[...].reshape(rows, 1024)
        weight = w[...].reshape(rows, 1024).astype(F32)
        change = 0.01 * first.astype(F32) / (jnp.sqrt(second.astype(F32)) + 1e-8)
        new_w[0] = (weight - change).astype(BF)
        new_m[0] = first
        new_q[0] = second


def shape(*dims, dtype=BF):
    return jax.ShapeDtypeStruct(dims, dtype)


def semaphores(groups):
    dma = pltpu.SemaphoreType.DMA
    return [
        dma((groups, 3, 3)),
        dma((groups, 3, 3)),
        dma((sum(SLOTS) * 3,)),
        dma((8,)),
        dma((4, 3, 3, 2)),
        dma((4, 3, 3)),
    ]


def bounce_buffers():
    return [
        pltpu.VMEM(bounce_shape(s, phase), BF)
        for phase in range(3)
        for _ in range(SLOTS[phase])
        for s in range(3)
    ]


def token_buffers(wide):
    return [(4, 2, 4, 48, n) for n in wide]


def constants():
    i = np.arange(192)
    swap = (i // 12 % 4 * 48 + i // 48 * 12 + i % 12)[:, None] == i[None, :]
    block = np.arange(4)[:, None, None]
    line = np.arange(16)[None, None, :]
    rows = i[None, :, None]
    pick = (rows // 12 % 4 == block) & (line // 4 == block) & (line % 4 == rows // 48)
    return (
        jnp.asarray(swap.astype(np.float32), BF),
        jnp.asarray(pick.reshape(768, 16).astype(np.float32), BF),
    )


def tables(old_experts, source):
    j = jnp.arange(N, dtype=jnp.int32)
    src = source.reshape(4, 4, 4, 2).transpose(0, 1, 3, 2).reshape(N)
    expert = jnp.sum(jnp.where(src[:, None] == j[None, :], old_experts[None, :], 0), axis=1)
    same = expert[:, None] == expert[None, :]
    before = jnp.max(jnp.where(same & (j[None, :] < j[:, None]), j[None, :], -1), axis=1)
    before = jnp.where(before < 0, N, before)
    last = jnp.max(jnp.where(same, j[None, :], -1), axis=1)
    x = (src // 2) % 4
    rows = [src // 32, (src // 8) % 4, src % 2] + [(x == k).astype(jnp.int32) for k in range(4)]
    return jnp.stack(rows + [before, last])


def shards(
    tokens,
    cotangent,
    routes,
    gate_weights,
    old_experts,
    source,
    gate_up_weight,
    down_weight,
    first_gate_up,
    first_down,
    second_gate_up,
    second_down,
):
    table = tables(old_experts, source)
    swap, pick = constants()
    gu_shape, dn_shape = (4, 4, 2, 32, 1024), BUF
    arrays = (
        gate_up_weight.reshape(gu_shape),
        down_weight.reshape(dn_shape),
        first_gate_up.reshape(gu_shape),
        first_down.reshape(dn_shape),
        second_gate_up.reshape(gu_shape),
        second_down.reshape(dn_shape),
    )
    smem = pl.BlockSpec(memory_space=pltpu.SMEM)
    vmem = pl.BlockSpec(memory_space=pltpu.VMEM)
    hbm = pl.BlockSpec(memory_space=pl.ANY)
    gu, buf = shape(*gu_shape), shape(*BUF)
    mega = 1 << 20
    outs = pl.pallas_call(
        step_kernel,
        out_shape=[shape(N, 1024)]
        + [gu, buf] * 3
        + [buf] * 48
        + [shape(*b) for wide in (X_WIDE, C_WIDE, Y_WIDE) for b in token_buffers(wide)],
        in_specs=[smem] + [vmem] * 6 + [hbm] * 6,
        out_specs=[vmem] + [hbm] * 63,
        scratch_shapes=[pltpu.VMEM(BUF, BF)] * 12
        + [
            pltpu.VMEM(b, BF)
            for wide in (X_WIDE, C_WIDE, X_WIDE, C_WIDE, Y_WIDE)
            for b in token_buffers(wide)
        ]
        + [pltpu.VMEM((4, 128, n), BF) for n in X_WIDE + C_WIDE + Y_WIDE]
        + [pltpu.VMEM(gu_shape, BF), pltpu.VMEM(BUF, BF)] * 2
        + [pltpu.VMEM((ROWS, 1024), BF)] * 2
        + [pltpu.VMEM((ROWS, 512), BF), pltpu.VMEM((ROWS, 1024), BF)]
        + [pltpu.VMEM((3, N + 1, 16, 256), F32)]
        + [pltpu.VMEM((3, 4, 8, N), jnp.int32), pltpu.VMEM((3, 4, 8, N), F32)]
        + [pltpu.VMEM((3, N, N), BF), pltpu.VMEM((3, 3, N, N), BF)]
        + [pltpu.VMEM((512, 384), F32), pltpu.VMEM((N, 1024), F32)]
        + semaphores(7)
        + bounce_buffers(),
        compiler_params=pltpu.CompilerParams(
            collective_id=0, has_side_effects=True, vmem_limit_bytes=63 * mega
        ),
    )(table, swap, pick, routes.T, gate_weights.T, tokens, cotangent, *arrays)
    layer_out, home_gu, home_dn, m_gu, m_dn, q_gu, q_dn = outs[:7]

    def pieces(rows):
        return pl.BlockSpec((1, 2, 2, rows, 1024), lambda i: (i // 2, i % 2, 0, 0, 0))

    def whole(rows):
        return pl.BlockSpec((1, rows, 1024), lambda i: (0, i, 0))

    new = pl.pallas_call(
        weights_kernel,
        grid=(8,),
        out_shape=[shape(1, 1024, 1024)] * 3 + [shape(1, 512, 1024)] * 3,
        in_specs=[pieces(32)] * 3 + [pieces(16)] * 3,
        out_specs=[whole(128)] * 3 + [whole(64)] * 3,
        compiler_params=pltpu.CompilerParams(vmem_limit_bytes=60 * mega),
    )(home_gu, m_gu, q_gu, home_dn, m_dn, q_dn)
    return layer_out, new[0], new[3], new[1], new[4], new[2], new[5]


def solution(mesh):
    tok = P("ep", None)
    slot = P("ep", None, None)
    return jax.shard_map(
        shards,
        mesh=mesh,
        in_specs=(tok,) * 4 + (P(), P()) + (slot,) * 6,
        out_specs=(tok,) + (slot,) * 6,
        check_vma=False,
    )
```
